32 devices in a mesh: replica: 4 (over x, core), shard: 8 (over z, y).
Axes of the slice: x: 2, y: 2, z: 4, core: 2. Of those that a mesh axis runs over, the one named last changes fastest.
Arguments:
- images: bfloat16 [128, 197, 768], P(('replica', 'shard')), may hold values from -6 to 6
- routes: int32 [128, 197, 2], P(('replica', 'shard')), may hold values from 0 to 7, all different within a row; in each aligned block of 788 rows (0 to 787, 788 to 1575, ..., all dimensions but the last counted through in order) at most 275 rows name the same one
- cotangent: bfloat16 [128, 197, 768], P(('replica', 'shard')), may hold values from -6 to 6
- ln1_gain: bfloat16 [768], P('shard'), may hold values from 0.5 to 1.5
- ln1_bias: bfloat16 [768], P('shard'), may hold values from -1.75 to 1.75
- qkv_weight: bfloat16 [768, 2304], P('shard'), may hold values from -0.21875 to 0.21875
- q_bias: bfloat16 [768], P('shard'), may hold values from -1.75 to 1.75
- v_bias: bfloat16 [768], P('shard'), may hold values from -1.75 to 1.75
- out_weight: bfloat16 [768, 768], P('shard'), may hold values from -1.25 to 1.25
- out_bias: bfloat16 [768], P('shard'), may hold values from -1.75 to 1.75
- ln2_gain: bfloat16 [768], P('shard'), may hold values from 0.5 to 1.5
- ln2_bias: bfloat16 [768], P('shard'), may hold values from -1.75 to 1.75
- router_weight: bfloat16 [768, 8], P('shard'), may hold values from -0.15625 to 0.15625
- expert_in: bfloat16 [8, 768, 3072], P('shard'), may hold values from -0.21875 to 0.21875
- expert_in_bias: bfloat16 [8, 3072], P('shard'), may hold values from -0.625 to 0.625
- expert_out: bfloat16 [8, 3072, 768], P('shard'), may hold values from -1.75 to 1.75
- expert_out_bias: bfloat16 [8, 768], P('shard'), may hold values from -6 to 6
Outputs:
- output: bfloat16 [128, 197, 768], P(('replica', 'shard'))
- input_grad: bfloat16 [128, 197, 768], P(('replica', 'shard'))
- ln1_gain_grad: float32 [768], P('shard')
- ln1_bias_grad: float32 [768], P('shard')
- qkv_weight_grad: float32 [768, 2304], P('shard')
- q_bias_grad: float32 [768], P('shard')
- v_bias_grad: float32 [768], P('shard')
- out_weight_grad: float32 [768, 768], P('shard')
- out_bias_grad: float32 [768], P('shard')
- ln2_gain_grad: float32 [768], P('shard')
- ln2_bias_grad: float32 [768], P('shard')
- router_weight_grad: float32 [768, 8], P('shard')
- expert_in_grad: float32 [8, 768, 3072], P('shard')
- expert_in_bias_grad: float32 [8, 3072], P('shard')
- expert_out_grad: float32 [8, 3072, 768], P('shard')
- expert_out_bias_grad: float32 [8, 768], P('shard')
The draws below stay inside these ranges and needn't reach their ends.
Inputs may be any that keep to these rules, and one draw needn't show every extreme that they name: `routes`: each token names two different experts. Within the rows of one device (aligned blocks of 788 tokens in image order) no expert is named by more than 275 copies, a bound that some block reaches.
All inputs are finite; a program needn't handle non-finite values.
Results may differ from the reference program's by a relative error of at most 0.022.
Values may be sent and summed in bfloat16 or wider, within the bound.
No kernel may reach another device: no remote copies, remote signals or barrier semaphores. Data moves between devices by JAX's collectives and lax.ppermute only.
A program may use at most 256 MiB of HBM per device.

```python
import math
import jax
import jax.numpy as jnp
import numpy as np
from jax import lax

D = 768
HEADS = 12
HEAD_DIM = 64
FF = 3072
SEQ = 197
IMG_DEV = 4
TOK_DEV = 788
IMAGES = 128
EXPERTS = 8
CAPACITY = 275
N_REPLICA = 4
N_SHARD = 8


def block_levels(rng, dims, cuts, low, high):
    gain = 1.0
    for position, blocks in cuts:
        steps = jax.random.uniform(jax.random.fold_in(jax.random.fold_in(rng, 6), position), (blocks,), jnp.float32, low / len(cuts), high / len(cuts))
        gain = gain * jnp.repeat(jnp.exp(steps), dims[position] // blocks).reshape((-1,) + (1,) * (len(dims) - 1 - position))
    return gain


def assign_block(stream_key, own, number, rows, count, top, limit, slope):
    sequence = jax.random.permutation(stream_key, count)
    crowded, ordinary = portions_of(count, rows * top, limit, slope, True), portions_of(count, rows * top, limit, slope, False)
    places = jnp.arange(count)

    def named(lengths, offset_by):
        used = int((lengths > 0).sum())
        fixed = max(1, used // 4)
        moved = fixed + (places - fixed + offset_by * (used - fixed)) % max(1, count - fixed)
        return jnp.zeros((count,), jnp.int32).at[sequence[jnp.where(places < fixed, places, moved)]].set(jnp.asarray(lengths, jnp.int32))

    lengths = jnp.where(number % 4 == 0, named(crowded, number // 4), named(ordinary, number - number // 4 - 1))
    mixed = jax.random.permutation(jax.random.fold_in(own, 3), count)
    source_of, receiver = mixed[0:count // 2 * 2:2], mixed[1:count // 2 * 2:2]
    margin = jnp.minimum(lengths[source_of] - 1, limit - lengths[receiver]) // 2
    margin = jnp.where((source_of == sequence[0]) | (receiver == sequence[0]) | (lengths[receiver] == 0), 0, jnp.maximum(margin, 0))
    moved = jax.random.randint(jax.random.fold_in(own, 4), (count // 2,), 0, 1 << 20) % (margin + 1)
    lengths = lengths.at[source_of].add(-moved).at[receiver].add(moved)
    labels = jnp.searchsorted(jnp.cumsum(lengths), jnp.arange(rows * top), side="right").astype(jnp.int32)
    grid = labels.reshape(top, rows).T
    grid = grid[jax.random.permutation(jax.random.fold_in(own, 1), rows)]
    offset_by = jax.random.randint(jax.random.fold_in(own, 2), (rows, 1), 0, top)
    return jnp.take_along_axis(grid, (jnp.arange(top)[None, :] + offset_by) % top, axis=1)


def portions_of(count, total, reach, skew, full):
    weights = [(1 << 20) // math.isqrt(grade ** skew) + 1 for grade in range(1, count + 1)]
    largest = reach if full else min(reach, max(-(-total // count), total * weights[0] // sum(weights)))
    least = 1 if total - largest >= count - 1 else 0
    counts, rest = [largest] + [least] * (count - 1), total - largest - least * (count - 1)
    while rest > 0:
        candidates = [i for i in range(1, count) if counts[i] < largest] or [i for i in range(1, count) if counts[i] < reach]
        whole, remaining = sum([weights[i] for i in candidates]), rest
        for i in candidates:
            more = min(reach - counts[i], max(1, remaining * weights[i] // whole), rest)
            counts[i] = counts[i] + more
            rest = rest - more
    return np.array(counts)


def bell_draw(own_key, dims, deviation, most, cuts=(), held_as=jnp.bfloat16):
    values = jax.random.normal(own_key, dims, jnp.float32) * deviation
    if len(cuts) > 0:
        values = block_levels(own_key, dims, cuts, -0.22, 0.18) * values
    return jnp.clip(values, min=-most, max=most).astype(held_as)


def setup_inputs(seed: int = 0) -> dict:
    key_of = jax.random.split(jax.random.key(seed), 18)
    images = bell_draw(key_of[0], (IMAGES, SEQ, D), 1.0, 6.0, ((0, 32),))
    routes_keys = jax.random.split(jax.random.fold_in(key_of[1], 1), IMAGES * SEQ // TOK_DEV)
    routes_turns = jax.random.permutation(jax.random.fold_in(key_of[1], 3), IMAGES * SEQ // TOK_DEV)
    routes = jax.vmap(lambda own, number: assign_block(jax.random.fold_in(key_of[1], 2), own, number, TOK_DEV, EXPERTS, 2, CAPACITY, 0))(routes_keys, routes_turns).reshape((IMAGES, SEQ, 2))
    cotangent = bell_draw(key_of[2], (IMAGES, SEQ, D), 1.0, 6.0, ((0, 32),))
    ln1_gain = jnp.clip(1.0 + 0.1 * jax.random.normal(key_of[3], (D,), jnp.float32), 0.5, 1.5).astype(jnp.bfloat16)
    ln1_bias = bell_draw(key_of[4], (D,), 0.3, 1.75, ((0, 8),))
    qkv_weight = bell_draw(key_of[5], (D, 3 * D), D ** -0.5, 0.21875, ((0, 8),))
    q_bias = bell_draw(key_of[6], (D,), 0.3, 1.75, ((0, 8),))
    v_bias = bell_draw(key_of[7], (D,), 0.3, 1.75, ((0, 8),))
    out_weight = bell_draw(key_of[8], (D, D), (D // 32) ** -0.5, 1.25, ((0, 8),))
    out_bias = bell_draw(key_of[9], (D,), 0.3, 1.75, ((0, 8),))
    ln2_gain = jnp.clip(1.0 + 0.1 * jax.random.normal(key_of[10], (D,), jnp.float32), 0.5, 1.5).astype(jnp.bfloat16)
    ln2_bias = bell_draw(key_of[11], (D,), 0.3, 1.75, ((0, 8),))
    router_weight = bell_draw(key_of[12], (D, EXPERTS), (2 * D) ** -0.5, 0.15625, ((0, 8),))
    expert_in = bell_draw(key_of[13], (EXPERTS, D, FF), D ** -0.5, 0.21875, ((0, 8),))
    expert_in_bias = bell_draw(key_of[14], (EXPERTS, FF), 0.1, 0.625, ((0, 8),))
    expert_out = bell_draw(key_of[15], (EXPERTS, FF, D), (max(FF // 256, 1)) ** -0.5, 1.75, ((0, 8),))
    expert_out_bias = bell_draw(key_of[16], (EXPERTS, D), 1.0, 6.0, ((0, 8),))
    return {"images": images, "routes": routes, "cotangent": cotangent, "ln1_gain": ln1_gain, "ln1_bias": ln1_bias, "qkv_weight": qkv_weight, "q_bias": q_bias, "v_bias": v_bias, "out_weight": out_weight, "out_bias": out_bias, "ln2_gain": ln2_gain, "ln2_bias": ln2_bias, "router_weight": router_weight, "expert_in": expert_in, "expert_in_bias": expert_in_bias, "expert_out": expert_out, "expert_out_bias": expert_out_bias}


eps_norm = 1e-06

@jax.custom_vjp
def low(v):
    return lax.optimization_barrier(v.astype(jnp.bfloat16)).astype(jnp.float32)

@jax.custom_vjp
def low_back(v):
    return v

def low_keep(v):
    return (low(v), None)

def low_pass(kept, grad):
    return (grad,)

def back_keep(v):
    return (v, None)

def back_low(kept, grad):
    return (low(grad),)
low.defvjp(low_keep, low_pass)
low_back.defvjp(back_keep, back_low)

def layer_norm(values, gain_vec, shift_vec):
    average = lax.optimization_barrier(jnp.mean(values, -1, keepdims=True))
    centred = values - average
    variance = lax.optimization_barrier(jnp.mean(centred * centred, -1, keepdims=True))
    return centred * lax.rsqrt(variance + eps_norm) * gain_vec + shift_vec

def slot_index(route_ids):
    flat_ids = route_ids.reshape(-1)
    onehot = (flat_ids[:, None] == jnp.arange(EXPERTS, dtype=jnp.int32)[None, :]).astype(jnp.int32)
    ranking = lax.optimization_barrier(jnp.sum((jnp.cumsum(onehot, 0) - 1) * onehot, 1))
    return (flat_ids * CAPACITY + ranking).astype(jnp.int32)

def block_forward(inputs, params, slot_ids, route_ids):
    gain_one, shift_one, qkv_full, query_bias, value_bias, out_full, out_shift, gain_two, shift_two, router_full, in_full, in_shift, outer_full, outer_shift = params
    highest = lax.Precision.HIGHEST
    row_values = inputs.reshape(TOK_DEV, D)
    normed = low(layer_norm(row_values, gain_one, shift_one))
    key_zeros = jnp.zeros((D,), jnp.float32)
    projected = jnp.dot(normed, qkv_full, precision=highest) + jnp.concatenate([query_bias, key_zeros, value_bias])
    projected = low(low_back(projected))
    heads_view = projected.reshape(IMG_DEV, SEQ, 3, HEADS, HEAD_DIM)
    queries = heads_view[:, :, 0]
    keys_all = heads_view[:, :, 1]
    values_all = heads_view[:, :, 2]
    scores = jnp.einsum('ishd,ithd->ihst', queries, keys_all, precision=highest) * HEAD_DIM ** (-0.5)
    scores = low_back(scores)
    attn_probs = jax.nn.softmax(scores, axis=-1)
    attended = jnp.einsum('ihst,ithd->ishd', low(attn_probs), values_all, precision=highest).reshape(TOK_DEV, D)
    attended = low(low_back(attended))
    branch = low_back(jnp.dot(attended, out_full, precision=highest) + out_shift)
    middle = row_values + branch
    normed_two = low(layer_norm(middle, gain_two, shift_two))
    logits = jnp.dot(normed_two, router_full, precision=highest)
    router_probs = jax.nn.softmax(logits, axis=-1)
    chosen = (route_ids[:, :, None] == jnp.arange(EXPERTS, dtype=jnp.int32)[None, None, :]).astype(jnp.float32)
    gate_values = lax.optimization_barrier(jnp.sum(router_probs[:, None, :] * chosen, -1))
    copies = jnp.broadcast_to(normed_two[:, None, :], (TOK_DEV, 2, D)).reshape(TOK_DEV * 2, D)
    copies = low_back(copies)
    buffer_rows = jnp.zeros((EXPERTS * CAPACITY, D), jnp.float32).at[slot_ids].set(copies)
    buffer_rows = buffer_rows.reshape(EXPERTS, CAPACITY, D)
    inner_act = jnp.einsum('ecd,edf->ecf', buffer_rows, in_full, precision=highest) + in_shift[:, None, :]
    inner_act = low_back(inner_act)
    hidden = low(jax.nn.gelu(inner_act))
    outer_act = jnp.einsum('ecf,efd->ecd', hidden, outer_full, precision=highest) + outer_shift[:, None, :]
    outer_act = low(low_back(outer_act))
    returned = outer_act.reshape(EXPERTS * CAPACITY, D)[slot_ids].reshape(TOK_DEV, 2, D)
    mixed_rows = middle + lax.optimization_barrier(jnp.sum(gate_values[:, :, None] * returned, 1))
    return mixed_rows.reshape(IMG_DEV, SEQ, D)

def add_pair(first, second):
    return first + second

def reference(images, routes, cotangent, ln1_gain, ln1_bias, qkv_weight, q_bias, v_bias, out_weight, out_bias, ln2_gain, ln2_bias, router_weight, expert_in, expert_in_bias, expert_out, expert_out_bias):
    weights = tuple((item.astype(jnp.float32) for item in (ln1_gain, ln1_bias, qkv_weight, q_bias, v_bias, out_weight, out_bias, ln2_gain, ln2_bias, router_weight, expert_in, expert_in_bias, expert_out, expert_out_bias)))
    blocks = N_REPLICA * N_SHARD
    image_blocks = images.astype(jnp.float32).reshape(blocks, IMG_DEV, SEQ, D)
    cot_blocks = cotangent.astype(jnp.float32).reshape(blocks, IMG_DEV, SEQ, D)
    route_blocks = routes.reshape(blocks, TOK_DEV, 2)

    def one_block(totals, pieces):
        block_images, block_cot, block_routes = pieces
        slot_ids = slot_index(block_routes)

        def forward(inputs, params):
            return block_forward(inputs, params, slot_ids, block_routes)
        result, pullback = jax.vjp(forward, block_images, weights)
        input_part, weight_part = pullback(block_cot)
        totals = jax.tree.map(add_pair, totals, weight_part)
        return (totals, (result.astype(jnp.bfloat16), input_part.astype(jnp.bfloat16)))
    initial = jax.tree.map(jnp.zeros_like, weights)
    totals, (outputs, input_grads) = lax.scan(one_block, initial, (image_blocks, cot_blocks, route_blocks))
    output = outputs.reshape(IMAGES, SEQ, D)
    input_grad = input_grads.reshape(IMAGES, SEQ, D)
    return (output, input_grad, totals[0], totals[1], totals[2], totals[3], totals[4], totals[5], totals[6], totals[7], totals[8], totals[9], totals[10], totals[11], totals[12], totals[13])
```

```python
import jax
import jax.numpy as jnp
from jax import lax
from jax.sharding import PartitionSpec as P

HEADS = 12
HEAD_DIM = 64
LANES = 128


eps_norm = 1e-06
f32 = jnp.float32
bf16 = jnp.bfloat16


def normalize(values):
    average = jnp.mean(values, -1, keepdims=True)
    centred = values - average
    variance = jnp.mean(centred * centred, -1, keepdims=True)
    inverse = lax.rsqrt(variance + eps_norm)
    return (centred * inverse, inverse)


def norm_back(grad_out, scaled, inverse, gain_vec):
    gain_grad = jnp.sum(grad_out * scaled, 0)
    shift_grad = jnp.sum(grad_out, 0)
    grad_scaled = grad_out * gain_vec
    first_term = jnp.mean(grad_scaled, -1, keepdims=True)
    second_term = jnp.mean(grad_scaled * scaled, -1, keepdims=True)
    return (inverse * (grad_scaled - first_term - scaled * second_term), gain_grad, shift_grad)


def slot_index(route_ids, experts, stride):
    flat_ids = route_ids.reshape(-1)
    onehot = (flat_ids[:, None] == jnp.arange(experts, dtype=jnp.int32)[None, :]).astype(jnp.int32)
    ranking = jnp.sum((jnp.cumsum(onehot, 0) - 1) * onehot, 1)
    return (flat_ids * stride + ranking).reshape(route_ids.shape)


def exchange(rows, experts):
    width = rows.shape[-1]
    blocks = rows.reshape(experts, rows.shape[0] // experts, width)
    moved = lax.all_to_all(blocks, "shard", split_axis=0, concat_axis=0, tiled=True)
    return moved.reshape(rows.shape)


def replica_sum(value):
    count = lax.axis_size("replica")
    me = lax.axis_index("replica")
    core = me % 2
    half = value.shape[0] // 2
    mine = lax.dynamic_slice_in_dim(value, core * half, half, 0)
    other = lax.dynamic_slice_in_dim(value, (1 - core) * half, half, 0)
    mine = mine.astype(f32) + lax.ppermute(
        other, "replica", [(i, i ^ 1) for i in range(count)]
    ).astype(f32)
    mine = mine.astype(bf16)
    step = 2
    while step < count:
        theirs = lax.ppermute(mine, "replica", [(i, i ^ step) for i in range(count)])
        mine = (mine.astype(f32) + theirs.astype(f32)).astype(bf16)
        step *= 2
    theirs = lax.ppermute(mine, "replica", [(i, i ^ 1) for i in range(count)])
    first = jnp.where(core == 0, mine, theirs).astype(f32)
    second = jnp.where(core == 0, theirs, mine).astype(f32)
    return jnp.concatenate([first, second], 0)


def per_device(
    images,
    routes,
    cotangent,
    ln1_gain,
    ln1_bias,
    qkv_weight,
    q_bias,
    v_bias,
    out_weight,
    out_bias,
    ln2_gain,
    ln2_bias,
    router_weight,
    expert_in,
    expert_in_bias,
    expert_out,
    expert_out_bias,
):
    experts = lax.axis_size("shard")
    expert_here = lax.axis_index("shard")
    images_here, seq_len, model_width = images.shape
    tokens_here = images_here * seq_len
    capacity = 14 * tokens_here // (5 * experts)
    stride = -(-capacity // 8) * 8
    slots = experts * stride
    factor = HEAD_DIM ** (-0.5)

    columns = [ln1_gain, ln1_bias, q_bias, v_bias, out_bias, ln2_gain, ln2_bias]
    small = jnp.concatenate([router_weight, jnp.stack(columns, 1)], 1)
    width_small = -(-small.shape[1] // LANES) * LANES
    small = jnp.pad(small, ((0, 0), (0, width_small - small.shape[1])))
    packed = lax.all_gather(
        jnp.concatenate([qkv_weight, out_weight, small], 1), "shard", axis=0, tiled=True
    )
    qkv_full = packed[:, : 3 * model_width]
    out_full = packed[:, 3 * model_width : 4 * model_width]
    small_full = packed[:, 4 * model_width :]
    router_full = small_full[:, :experts]
    vectors = small_full[:, experts : experts + len(columns)].T.astype(f32)
    gain_one, shift_one, query_bias, value_bias, out_shift, gain_two, shift_two = vectors

    route_rows = routes.reshape(tokens_here, 2)
    slot_ids = slot_index(route_rows, experts, stride)
    slot_row = jnp.arange(slots, dtype=jnp.int32)
    send = (
        (slot_row[:, None] == slot_ids[None, :, 0]) | (slot_row[:, None] == slot_ids[None, :, 1])
    ).astype(bf16)
    collect = (
        (slot_ids[:, 0, None] == slot_row[None, :]) | (slot_ids[:, 1, None] == slot_row[None, :])
    ).astype(bf16)

    cot_rows = cotangent.reshape(tokens_here, model_width)
    cot_sent = jnp.dot(send, cot_rows, preferred_element_type=f32).astype(bf16)
    cot_there = exchange(cot_sent, experts)

    row_values = images.reshape(tokens_here, model_width).astype(f32)
    scaled_one, inverse_one = normalize(row_values)
    normed = (scaled_one * gain_one + shift_one).astype(bf16)
    qkv_shift = jnp.concatenate([query_bias, jnp.zeros((model_width,), f32), value_bias])
    projected = (jnp.dot(normed, qkv_full, preferred_element_type=f32) + qkv_shift).astype(bf16)
    heads_view = projected.reshape(images_here, seq_len, 3, HEADS, HEAD_DIM)
    queries = heads_view[:, :, 0]
    keys_all = heads_view[:, :, 1]
    values_all = heads_view[:, :, 2]
    scores = (
        jnp.einsum("ishd,ithd->ihst", queries, keys_all, preferred_element_type=f32) * factor
    )
    row_max = jnp.max(scores, -1, keepdims=True)
    exp_scores = jnp.exp(scores - row_max)
    row_total = jnp.sum(exp_scores, -1, keepdims=True)
    attn_probs = exp_scores / row_total
    log_total = row_max + jnp.log(row_total)
    attended = jnp.einsum(
        "ihst,ithd->ishd", attn_probs.astype(bf16), values_all, preferred_element_type=f32
    )
    attended = attended.reshape(tokens_here, model_width).astype(bf16)
    middle = row_values + jnp.dot(attended, out_full, preferred_element_type=f32) + out_shift
    scaled_two, inverse_two = normalize(middle)
    normed_two = (scaled_two * gain_two + shift_two).astype(bf16)

    sent = jnp.dot(send, normed_two, preferred_element_type=f32).astype(bf16)
    arrived = exchange(sent, experts)

    probs = jax.nn.softmax(jnp.dot(arrived, router_full, preferred_element_type=f32), axis=-1)
    is_here = (jnp.arange(experts, dtype=jnp.int32) == expert_here).astype(f32)[None, :]
    gate = jnp.sum(probs * is_here, -1, keepdims=True)
    weight_in = expert_in[0]
    weight_out = expert_out[0]
    inner_act = jnp.dot(arrived, weight_in, preferred_element_type=f32) + expert_in_bias[0].astype(
        f32
    )
    hidden = jax.nn.gelu(inner_act).astype(bf16)
    outer_act = jnp.dot(hidden, weight_out, preferred_element_type=f32) + expert_out_bias[0].astype(
        f32
    )
    gated = (gate * outer_act).astype(bf16)
    cot_wide = cot_there.astype(f32)
    gate_grad = jnp.sum(cot_wide * outer_act, -1, keepdims=True)
    outer_grad = (gate * cot_wide).astype(bf16)
    logit_grads = gate_grad * gate * (is_here - probs)
    hidden_grad = jnp.einsum("rd,fd->rf", outer_grad, weight_out, preferred_element_type=f32)
    gelu_pull = jax.vjp(jax.nn.gelu, inner_act)[1]
    inner_grad = gelu_pull(hidden_grad)[0].astype(bf16)
    arrived_grad = (
        jnp.einsum("rf,df->rd", inner_grad, weight_in, preferred_element_type=f32)
        + jnp.einsum("re,de->rd", logit_grads, router_full.astype(f32))
    ).astype(bf16)
    back = exchange(arrived_grad, experts)
    returned = exchange(gated, experts)

    expert_out_part = jnp.einsum("rf,rd->fd", hidden, outer_grad, preferred_element_type=f32)
    expert_out_grad = replica_sum(expert_out_part.astype(bf16))[None]
    expert_in_part = jnp.einsum("rd,rf->df", arrived, inner_grad, preferred_element_type=f32)
    expert_in_grad = replica_sum(expert_in_part.astype(bf16))[None]
    expert_out_bias_part = jnp.sum(outer_grad.astype(f32), 0)
    expert_in_bias_part = jnp.sum(inner_grad.astype(f32), 0)
    router_grad = jnp.einsum("rd,re->de", arrived.astype(f32), logit_grads)

    grad_out = cot_rows.astype(f32)
    normed_two_grad = jnp.dot(collect, back, preferred_element_type=f32)
    middle_norm_grad, gain_two_grad, shift_two_grad = norm_back(
        normed_two_grad, scaled_two, inverse_two, gain_two
    )
    middle_grad = grad_out + middle_norm_grad
    branch_grad = middle_grad.astype(bf16)
    out_shift_grad = jnp.sum(branch_grad.astype(f32), 0)
    out_full_grad = jnp.einsum("td,te->de", attended, branch_grad, preferred_element_type=f32)
    attended_grad = jnp.einsum(
        "te,de->td", branch_grad, out_full, preferred_element_type=f32
    ).astype(bf16)
    grad_heads = attended_grad.reshape(images_here, seq_len, HEADS, HEAD_DIM)
    scores_back = (
        jnp.einsum("ishd,ithd->ihst", queries, keys_all, preferred_element_type=f32) * factor
    )
    probs_back = jnp.exp(scores_back - log_total)
    values_grad = jnp.einsum(
        "ihst,ishd->ithd", probs_back.astype(bf16), grad_heads, preferred_element_type=f32
    )
    prob_back_grad = jnp.einsum(
        "ishd,ithd->ihst", grad_heads, values_all, preferred_element_type=f32
    )
    score_grad = (
        probs_back * (prob_back_grad - jnp.sum(probs_back * prob_back_grad, -1, keepdims=True))
    ).astype(bf16)
    query_grad = (
        jnp.einsum("ihst,ithd->ishd", score_grad, keys_all, preferred_element_type=f32) * factor
    )
    key_grad = (
        jnp.einsum("ihst,ishd->ithd", score_grad, queries, preferred_element_type=f32) * factor
    )
    projected_grad = (
        jnp.stack([query_grad, key_grad, values_grad], 2)
        .reshape(tokens_here, 3 * model_width)
        .astype(bf16)
    )
    qkv_full_grad = jnp.einsum("td,te->de", normed, projected_grad, preferred_element_type=f32)
    projected_sums = jnp.sum(projected_grad.astype(f32), 0)
    query_bias_grad = projected_sums[:model_width]
    value_bias_grad = projected_sums[2 * model_width :]
    normed_grad = jnp.einsum("te,de->td", projected_grad, qkv_full, preferred_element_type=f32)
    rows_norm_grad, gain_one_grad, shift_one_grad = norm_back(
        normed_grad, scaled_one, inverse_one, gain_one
    )
    output = (
        (middle + jnp.dot(collect, returned, preferred_element_type=f32))
        .reshape(images.shape)
        .astype(bf16)
    )
    input_grad = (middle_grad + rows_norm_grad).astype(bf16).reshape(images.shape)

    vector_grads = [
        gain_one_grad,
        shift_one_grad,
        query_bias_grad,
        value_bias_grad,
        out_shift_grad,
        gain_two_grad,
        shift_two_grad,
    ]
    small_grad = jnp.concatenate([router_grad.T, jnp.stack(vector_grads, 0)], 0)
    small_grad = jnp.pad(small_grad, ((0, width_small - small_grad.shape[0]), (0, 0)))
    packed_grad = jnp.concatenate(
        [qkv_full_grad.astype(bf16), out_full_grad.astype(bf16), small_grad.T.astype(bf16)], 1
    )
    owned = lax.psum_scatter(packed_grad, "shard", scatter_dimension=0, tiled=True)
    bias_parts = jnp.concatenate([expert_in_bias_part, expert_out_bias_part]).astype(bf16)
    width_all = owned.shape[1]
    bias_rows = -(-bias_parts.shape[0] // width_all)
    bias_parts = jnp.pad(bias_parts, (0, bias_rows * width_all - bias_parts.shape[0]))
    owned = jnp.concatenate([owned, bias_parts.reshape(bias_rows, width_all)], 0)
    summed = lax.psum(owned, "replica").astype(f32)
    rows = qkv_weight.shape[0]
    biases = summed[rows:].reshape(-1)
    hidden_width = expert_in_bias.shape[1]
    summed = summed[:rows]
    small_sum = summed[:, 4 * model_width :]
    vector_sums = small_sum[:, experts : experts + len(columns)].T
    return (
        output,
        input_grad,
        vector_sums[0],
        vector_sums[1],
        summed[:, : 3 * model_width],
        vector_sums[2],
        vector_sums[3],
        summed[:, 3 * model_width : 4 * model_width],
        vector_sums[4],
        vector_sums[5],
        vector_sums[6],
        small_sum[:, :experts],
        expert_in_grad,
        biases[None, :hidden_width],
        expert_out_grad,
        biases[None, hidden_width : hidden_width + model_width],
    )


def solution(mesh):
    return jax.shard_map(
        per_device,
        mesh=mesh,
        in_specs=(
            P(("replica", "shard"), None, None),
            P(("replica", "shard"), None, None),
            P(("replica", "shard"), None, None),
            P("shard"),
            P("shard"),
            P("shard", None),
            P("shard"),
            P("shard"),
            P("shard", None),
            P("shard"),
            P("shard"),
            P("shard"),
            P("shard", None),
            P("shard", None, None),
            P("shard", None),
            P("shard", None, None),
            P("shard", None),
        ),
        out_specs=(
            P(("replica", "shard"), None, None),
            P(("replica", "shard"), None, None),
            P("shard"),
            P("shard"),
            P("shard", None),
            P("shard"),
            P("shard"),
            P("shard", None),
            P("shard"),
            P("shard"),
            P("shard"),
            P("shard", None),
            P("shard", None, None),
            P("shard", None),
            P("shard", None, None),
            P("shard", None),
        ),
        check_vma=False,
    )
```

```python
import functools

import jax
import jax.numpy as jnp
from jax import lax
from jax.experimental import pallas as pl
from jax.experimental.pallas import tpu as pltpu
from jax.sharding import PartitionSpec as P

HEADS = 12
HEAD_DIM = 64
LANES = 128
VMEM_BYTES = 56 * 1024 * 1024


eps_norm = 1e-06
f32 = jnp.float32
bf16 = jnp.bfloat16

GAIN_ONE, SHIFT_ONE, QUERY_BIAS, VALUE_BIAS, OUT_SHIFT, GAIN_TWO, SHIFT_TWO = range(7)
VECTORS = 7


def round_up(value, multiple):
    return -(-value // multiple) * multiple


def normalize(values):
    average = jnp.mean(values, -1, keepdims=True)
    centred = values - average
    variance = jnp.mean(centred * centred, -1, keepdims=True)
    inverse = lax.rsqrt(variance + eps_norm)
    return (centred * inverse, inverse)


def norm_back(grad_out, scaled, inverse, gain_vec):
    gain_grad = jnp.sum(grad_out * scaled, 0, keepdims=True)
    shift_grad = jnp.sum(grad_out, 0, keepdims=True)
    grad_scaled = grad_out * gain_vec
    first_term = jnp.mean(grad_scaled, -1, keepdims=True)
    second_term = jnp.mean(grad_scaled * scaled, -1, keepdims=True)
    return (inverse * (grad_scaled - first_term - scaled * second_term), gain_grad, shift_grad)


def dot(left, right):
    return jnp.dot(left, right, preferred_element_type=f32)


def dot_last(left, right):
    return lax.dot_general(left, right, (((1,), (1,)), ((), ())), preferred_element_type=f32)


def dot_first(left, right):
    return lax.dot_general(left, right, (((0,), (0,)), ((), ())), preferred_element_type=f32)


def params(steps=0):
    return pltpu.CompilerParams(
        vmem_limit_bytes=VMEM_BYTES,
        dimension_semantics=("arbitrary",) * steps if steps else None,
    )


def cost():
    return pl.CostEstimate(flops=1 << 20, bytes_accessed=1 << 16, transcendentals=0)


def whole(shape):
    return pl.BlockSpec(shape, lambda *_: (0,) * len(shape))


def scalar_spec():
    return pl.BlockSpec(memory_space=pltpu.SMEM)


def forward_kernel(seq_len, width, x_ref, w_ref, vec_ref, h1_ref, qkv_ref, o_ref, mid_ref, h2_ref):
    vec = vec_ref[...]

    def row(index):
        return vec[index : index + 1]

    x = x_ref[0].astype(f32)
    scaled, _ = normalize(x)
    h1 = (scaled * row(GAIN_ONE) + row(SHIFT_ONE)).astype(bf16)
    h1_ref[0] = h1
    for part, bias in ((0, QUERY_BIAS), (1, None), (2, VALUE_BIAS)):
        block = dot(h1, w_ref[:, part * width : (part + 1) * width])
        if bias is not None:
            block = block + row(bias)
        qkv_ref[0, :, part * width : (part + 1) * width] = block.astype(bf16)
    rows = x.shape[0]
    lane = lax.broadcasted_iota(jnp.int32, (1, LANES), 1)
    key_there = lax.broadcasted_iota(jnp.int32, (1, rows), 1) < seq_len
    factor = HEAD_DIM ** (-0.5)
    for pair in range(width // LANES):
        at = pair * LANES
        queries = qkv_ref[0, :, at : at + LANES] * jnp.asarray(factor, bf16)
        keys = qkv_ref[0, :, width + at : width + at + LANES]
        values = qkv_ref[0, :, 2 * width + at : 2 * width + at + LANES]
        total = None
        for half in range(LANES // HEAD_DIM):
            mine = (lane // HEAD_DIM) == half
            scores = dot_last(jnp.where(mine, queries, jnp.zeros_like(queries)), keys)
            scores = jnp.where(key_there, scores, -1e30)
            powers = jnp.exp(scores - jnp.max(scores, -1, keepdims=True))
            probs = (powers * (1.0 / jnp.sum(powers, -1, keepdims=True))).astype(bf16)
            part = dot(probs, jnp.where(mine, values, jnp.zeros_like(values)))
            total = part if total is None else total + part
        o_ref[0, :, at : at + LANES] = total.astype(bf16)
    middle = x + (dot(o_ref[0], w_ref[:, 3 * width : 4 * width]) + row(OUT_SHIFT))
    mid_ref[0] = middle
    scaled, _ = normalize(middle)
    h2_ref[0] = (scaled * row(GAIN_TWO) + row(SHIFT_TWO)).astype(bf16)


def attention_forward(x, packed, vec, seq_len):
    images, rows, width = x.shape

    def spec(columns):
        return pl.BlockSpec((1, rows, columns), lambda i: (i, 0, 0))

    def shape(columns, dtype):
        return jax.ShapeDtypeStruct((images, rows, columns), dtype)

    return pl.pallas_call(
        functools.partial(forward_kernel, seq_len, width),
        grid=(images,),
        in_specs=[spec(width), whole(packed.shape), whole(vec.shape)],
        out_specs=[spec(width), spec(3 * width), spec(width), spec(width), spec(width)],
        out_shape=[
            shape(width, bf16),
            shape(3 * width, bf16),
            shape(width, bf16),
            shape(width, f32),
            shape(width, bf16),
        ],
        compiler_params=params(1),
        cost_estimate=cost(),
        name="attention_forward",
    )(x, packed, vec)


def dispatch_kernel(slot_ref, rows_ref, out_ref):
    slots = slot_ref[...]
    high = out_ref.shape[0]
    slot = lax.broadcasted_iota(jnp.int32, (high, rows_ref.shape[0]), 0) + pl.program_id(0) * high
    hot = jnp.where((slot == slots[0:1]) | (slot == slots[1:2]), 1.0, 0.0).astype(bf16)
    out_ref[...] = dot(hot, rows_ref[...]).astype(bf16)


def dispatch(slots, rows, places, steps):
    width = rows.shape[1]
    return pl.pallas_call(
        dispatch_kernel,
        in_specs=[whole(slots.shape), whole(rows.shape)],
        out_specs=pl.BlockSpec((places // steps, width), lambda e: (e, 0)),
        grid=(steps,),
        out_shape=jax.ShapeDtypeStruct((places, width), bf16),
        compiler_params=params(1),
        cost_estimate=cost(),
        name="dispatch",
    )(slots, rows)


def expert_kernel(
    experts,
    tiles,
    here_ref,
    rows_ref,
    cot_ref,
    in_ref,
    in_bias_ref,
    out_ref,
    out_bias_ref,
    router_ref,
    back_ref,
    gated_ref,
    hidden_ref,
    inner_ref,
    outer_ref,
    logit_ref,
    in_sum_ref,
    out_sum_ref,
    slope_ref,
    total_ref,
):
    phase, tile = pl.program_id(0), pl.program_id(1)

    @pl.when(phase == 0)
    def _():
        act = dot(rows_ref[...], in_ref[0]) + in_bias_ref[...].astype(f32)
        square = act * act
        slant = 0.7978845608028654
        bend = jnp.tanh(act * (slant + (slant * 0.044715) * square))
        half = 0.5 + 0.5 * bend
        hidden = (act * half).astype(bf16)
        hidden_ref[...] = hidden
        slope_ref[tile] = half + (0.5 * act) * (1.0 - bend * bend) * (
            slant + (3.0 * slant * 0.044715) * square
        )
        part = dot(hidden, out_ref[0])

        @pl.when(tile == 0)
        def _():
            total_ref[...] = part

        @pl.when(tile > 0)
        def _():
            total_ref[...] += part

    @pl.when((phase == 0) & (tile == tiles - 1))
    def _():
        outer = total_ref[...] + out_bias_ref[...].astype(f32)
        logits = dot(rows_ref[...], router_ref[...])
        lane = lax.broadcasted_iota(jnp.int32, (1, LANES), 1)
        logits = jnp.where(lane < experts, logits, -1e30)
        powers = jnp.exp(logits - jnp.max(logits, -1, keepdims=True))
        probs = powers / jnp.sum(powers, -1, keepdims=True)
        is_here = jnp.where(lane == here_ref[0], 1.0, 0.0)
        gate = jnp.sum(probs * is_here, -1, keepdims=True)
        gated_ref[...] = (gate * outer).astype(bf16)
        cot = cot_ref[...].astype(f32)
        gate_grad = jnp.sum(cot * outer, -1, keepdims=True)
        outer_grad = (gate * cot).astype(bf16)
        outer_ref[...] = outer_grad
        out_sum_ref[...] = jnp.sum(outer_grad.astype(f32), 0, keepdims=True)
        logit_ref[...] = ((gate_grad * gate) * (is_here - probs)).astype(bf16)

    @pl.when(phase == 1)
    def _():
        hidden_grad = dot_last(outer_ref[...], out_ref[0])
        inner = (hidden_grad * slope_ref[tile]).astype(bf16)
        inner_ref[...] = inner
        in_sum_ref[...] = jnp.sum(inner.astype(f32), 0, keepdims=True)
        part = dot_last(inner, in_ref[0])

        @pl.when(tile == 0)
        def _():
            total_ref[...] = part + dot_last(logit_ref[...], router_ref[...])

        @pl.when(tile > 0)
        def _():
            total_ref[...] += part

    @pl.when((phase == 1) & (tile == tiles - 1))
    def _():
        back_ref[...] = total_ref[...].astype(bf16)


def expert_chunk(here, rows_in, cots, weights, router, experts):
    rows, width = rows_in.shape
    weight_in, bias_in, weight_out, bias_out = weights
    hidden = weight_in.shape[2]
    depth = 512
    tiles = hidden // depth

    def first_phase(p, f, _):
        return (0, jnp.where(p == 0, f, tiles - 1))

    def second_phase(p, f, _):
        return (0, jnp.where(p == 0, 0, f))

    every = whole((rows, width))

    def shape(columns):
        return jax.ShapeDtypeStruct((rows, columns), bf16)

    return pl.pallas_call(
        functools.partial(expert_kernel, experts, tiles),
        grid_spec=pltpu.PrefetchScalarGridSpec(
            num_scalar_prefetch=1,
            grid=(2, tiles),
            in_specs=[
                every,
                every,
                pl.BlockSpec((1, width, depth), lambda p, f, _: (0, 0, f)),
                pl.BlockSpec((1, depth), lambda p, f, _: (0, f)),
                pl.BlockSpec((1, depth, width), lambda p, f, _: (0, f, 0)),
                whole((1, width)),
                whole(router.shape),
            ],
            out_specs=[
                every,
                every,
                pl.BlockSpec((rows, depth), first_phase),
                pl.BlockSpec((rows, depth), second_phase),
                every,
                whole((rows, LANES)),
                pl.BlockSpec((1, depth), second_phase),
                whole((1, width)),
            ],
            scratch_shapes=[
                pltpu.VMEM((tiles, rows, depth), f32),
                pltpu.VMEM((rows, width), f32),
            ],
        ),
        out_shape=[
            shape(width),
            shape(width),
            shape(hidden),
            shape(hidden),
            shape(width),
            shape(LANES),
            jax.ShapeDtypeStruct((1, hidden), f32),
            jax.ShapeDtypeStruct((1, width), f32),
        ],
        compiler_params=params(2),
        cost_estimate=cost(),
        name="expert_chunk",
    )(here, rows_in, cots, weight_in, bias_in, weight_out, bias_out, router)


def out_grad_kernel(parts, core_ref, *refs):
    hidden_refs, outer_refs = refs[:parts], refs[parts : 2 * parts]
    mine_ref, other_ref = refs[2 * parts : 2 * parts + 2]
    turned_refs = refs[2 * parts + 2 :]
    step = pl.program_id(0)

    @pl.when(step == 0)
    def _():
        for outer_ref, turned_ref in zip(outer_refs, turned_refs):
            turned_ref[...] = outer_ref[...].T

    total = sum(dot(turned[...], hidden[...]) for turned, hidden in zip(turned_refs, hidden_refs))
    block = total.astype(bf16).T

    @pl.when(step < pl.num_programs(0) // 2)
    def _():
        other_ref[...] = block

    @pl.when(step >= pl.num_programs(0) // 2)
    def _():
        mine_ref[...] = block


def out_grad(core, hiddens, outers):
    parts = len(hiddens)
    high, wide = hiddens[0].shape[1], outers[0].shape[1]
    tile = 512
    half = high // 2 // tile

    def place(i, core_ref):
        own = i >= half
        return (0, jnp.where(own, core_ref[0], 1 - core_ref[0]) * half + i - own * half)

    return pl.pallas_call(
        functools.partial(out_grad_kernel, parts),
        grid_spec=pltpu.PrefetchScalarGridSpec(
            num_scalar_prefetch=1,
            grid=(2 * half,),
            in_specs=[pl.BlockSpec((rows.shape[0], tile), place) for rows in hiddens]
            + [whole(rows.shape) for rows in outers],
            out_specs=[
                pl.BlockSpec((tile, wide), lambda i, _: (jnp.maximum(i - half, 0), 0)),
                pl.BlockSpec((tile, wide), lambda i, _: (jnp.minimum(i, half - 1), 0)),
            ],
            scratch_shapes=[pltpu.VMEM((wide, rows.shape[0]), bf16) for rows in outers],
        ),
        out_shape=[jax.ShapeDtypeStruct((high // 2, wide), bf16)] * 2,
        compiler_params=params(1),
        cost_estimate=cost(),
        name="out_grad",
    )(core, *hiddens, *outers)


def in_grad_kernel(parts, core_ref, *refs):
    arrived_refs, inner_refs, logit_refs = (refs[i * parts : (i + 1) * parts] for i in range(3))
    mine_ref, other_ref, router_ref = refs[3 * parts : 3 * parts + 3]
    turned_refs = refs[3 * parts + 3 :]
    half = mine_ref.shape[0]

    @pl.when(pl.program_id(0) == 0)
    def _():
        for arrived_ref, turned_ref in zip(arrived_refs, turned_refs):
            turned = arrived_ref[...].T
            turned_ref[0] = turned[:half]
            turned_ref[1] = turned[half:]
        for h in range(2):
            router_ref[h * half : (h + 1) * half, :] = sum(
                dot(turned[h], logit[...]) for turned, logit in zip(turned_refs, logit_refs)
            )

    core = core_ref[0]
    mine_ref[...] = sum(
        dot(turned[core], inner[...]) for turned, inner in zip(turned_refs, inner_refs)
    ).astype(bf16)
    other_ref[...] = sum(
        dot(turned[1 - core], inner[...]) for turned, inner in zip(turned_refs, inner_refs)
    ).astype(bf16)


def in_grad(core, arrived, inners, logits):
    parts = len(inners)
    high, wide = arrived[0].shape[1], inners[0].shape[1]
    tile = 512
    spec = pl.BlockSpec((high // 2, tile), lambda i, _: (0, i))
    return pl.pallas_call(
        functools.partial(in_grad_kernel, parts),
        grid_spec=pltpu.PrefetchScalarGridSpec(
            num_scalar_prefetch=1,
            grid=(wide // tile,),
            in_specs=[whole(rows.shape) for rows in arrived]
            + [pl.BlockSpec((rows.shape[0], tile), lambda i, _: (0, i)) for rows in inners]
            + [whole(rows.shape) for rows in logits],
            out_specs=[spec, spec, whole((high, LANES))],
            scratch_shapes=[pltpu.VMEM((2, high // 2, rows.shape[0]), bf16) for rows in arrived],
        ),
        out_shape=[jax.ShapeDtypeStruct((high // 2, wide), bf16)] * 2
        + [jax.ShapeDtypeStruct((high, LANES), f32)],
        compiler_params=params(1),
        cost_estimate=cost(),
        name="in_grad",
    )(core, *arrived, *inners, *logits)


def widen_kernel(core_ref, mine_ref, theirs_ref, out_ref):
    own = pl.program_id(0) == core_ref[0]

    @pl.when(own)
    def _():
        out_ref[...] = mine_ref[...].astype(f32)

    @pl.when(jnp.logical_not(own))
    def _():
        out_ref[...] = theirs_ref[...].astype(f32)


def widen(core, mine, theirs):
    high, wide = mine.shape
    tile = high // 4

    def block(is_mine):
        def index(h, i, core_ref):
            used = (h == core_ref[0]) == is_mine
            return (jnp.where(used, i, 0), 0)

        return pl.BlockSpec((tile, wide), index)

    return pl.pallas_call(
        widen_kernel,
        grid_spec=pltpu.PrefetchScalarGridSpec(
            num_scalar_prefetch=1,
            grid=(2, 4),
            in_specs=[block(True), block(False)],
            out_specs=pl.BlockSpec((tile, wide), lambda h, i, _: (h * 4 + i, 0)),
        ),
        out_shape=jax.ShapeDtypeStruct((2 * high, wide), f32),
        compiler_params=params(2),
        cost_estimate=cost(),
        name="widen",
    )(core, mine, theirs)


def collect(slots, rows):
    slot = lax.broadcasted_iota(jnp.int32, (1, rows.shape[0]), 1)
    hot = (slots[:, 0:1] == slot) | (slots[:, 1:2] == slot)
    return dot(jnp.where(hot, 1.0, 0.0).astype(bf16), rows)


def collect_parts(slots, part_refs):
    return sum(
        collect(slots[:, 2 * part : 2 * part + 2], part_ref[...])
        for part, part_ref in enumerate(part_refs)
    )


def output_kernel(slot_ref, mid_ref, *refs):
    refs[-1][0] = (mid_ref[0] + collect_parts(slot_ref[0].T, refs[:-1])).astype(bf16)


def combine_output(image_slots, middle, returned):
    images, rows, width = middle.shape
    spec = pl.BlockSpec((1, rows, width), lambda i: (i, 0, 0))
    return pl.pallas_call(
        output_kernel,
        grid=(images,),
        in_specs=[pl.BlockSpec((1, *image_slots.shape[1:]), lambda i: (i, 0, 0)), spec]
        + [whole(part.shape) for part in returned],
        out_specs=spec,
        out_shape=jax.ShapeDtypeStruct((images, rows, width), bf16),
        compiler_params=params(1),
        cost_estimate=cost(),
        name="combine_output",
    )(image_slots, middle, *returned)


def backward_kernel(seq_len, width, experts, parts, core_ref, *refs):
    slot_ref, x_ref, cot_ref, mid_ref, qkv_ref, w_ref, vec_ref = refs[:7]
    h1_ref, o_ref, router_ref = refs[7:10]
    part_refs = refs[10 : 10 + parts]
    grad_ref, mine_ref, other_ref, dqkv_ref, sums_ref, total_ref = refs[10 + parts :]
    vec = vec_ref[...]

    def row(index):
        return vec[index : index + 1]

    h2_grad = collect_parts(slot_ref[0].T, part_refs)
    scaled, inverse = normalize(mid_ref[0])
    norm_grad, gain_two_grad, shift_two_grad = norm_back(h2_grad, scaled, inverse, row(GAIN_TWO))
    mid_grad = cot_ref[0].astype(f32) + norm_grad
    branch = mid_grad.astype(bf16)
    out_shift_grad = jnp.sum(branch.astype(f32), 0, keepdims=True)
    o_grad = dot_last(branch, w_ref[:, 3 * width : 4 * width]).astype(bf16)

    rows = branch.shape[0]
    lane = lax.broadcasted_iota(jnp.int32, (1, LANES), 1)
    key_there = lax.broadcasted_iota(jnp.int32, (rows, 1), 0) < seq_len
    factor = HEAD_DIM ** (-0.5)
    for pair in range(width // LANES):
        at = pair * LANES
        queries = qkv_ref[0, :, at : at + LANES] * jnp.asarray(factor, bf16)
        keys = qkv_ref[0, :, width + at : width + at + LANES]
        values = qkv_ref[0, :, 2 * width + at : 2 * width + at + LANES]
        grads = o_grad[:, at : at + LANES]
        query_grad = key_grad = value_grad = None
        for half in range(LANES // HEAD_DIM):
            mine = (lane // HEAD_DIM) == half

            def only(slab):
                return jnp.where(mine, slab, jnp.zeros_like(slab))

            own_queries, own_keys, own_grads = only(queries), only(keys), only(grads)
            scores = dot_last(own_keys, queries)
            scores = jnp.where(key_there, scores, -1e30)
            powers = jnp.exp(scores - jnp.max(scores, 0, keepdims=True))
            probs = powers * (1.0 / jnp.sum(powers, 0, keepdims=True))
            prob_grad = dot_last(values, own_grads)
            spread = jnp.sum(probs * prob_grad, 0, keepdims=True)
            score_grad = (probs * (prob_grad - spread)).astype(bf16)
            value_part = dot(probs.astype(bf16), own_grads)
            key_part = dot(score_grad, own_queries)
            query_part = dot_first(score_grad, own_keys)
            if half == 0:
                query_grad, key_grad, value_grad = query_part, key_part, value_part
            else:
                query_grad += query_part
                key_grad += key_part
                value_grad += value_part
        dqkv_ref[:, at : at + LANES] = (query_grad * factor).astype(bf16)
        dqkv_ref[:, width + at : width + at + LANES] = key_grad.astype(bf16)
        dqkv_ref[:, 2 * width + at : 2 * width + at + LANES] = value_grad.astype(bf16)

    h1_grad = dot_last(dqkv_ref[...], w_ref[:, : 3 * width])
    query_sum = jnp.sum(dqkv_ref[:, :width].astype(f32), 0, keepdims=True)
    value_sum = jnp.sum(dqkv_ref[:, 2 * width :].astype(f32), 0, keepdims=True)
    scaled, inverse = normalize(x_ref[0].astype(f32))
    norm_grad, gain_one_grad, shift_one_grad = norm_back(h1_grad, scaled, inverse, row(GAIN_ONE))
    grad_ref[0] = (mid_grad + norm_grad).astype(bf16)
    sums = [
        gain_one_grad,
        shift_one_grad,
        query_sum,
        value_sum,
        out_shift_grad,
        gain_two_grad,
        shift_two_grad,
        jnp.zeros((sums_ref.shape[0] - VECTORS, width), f32),
    ]
    sums = jnp.concatenate(sums, 0)

    image = pl.program_id(0)
    qkv_part = dot_first(h1_ref[0], dqkv_ref[...])
    out_part = dot_first(o_ref[0], branch)

    @pl.when(image == 0)
    def _():
        sums_ref[...] = sums
        total_ref[:, : 3 * width] = qkv_part
        total_ref[:, 3 * width : 4 * width] = out_part

    @pl.when(image > 0)
    def _():
        sums_ref[...] += sums
        total_ref[:, : 3 * width] += qkv_part
        total_ref[:, 3 * width : 4 * width] += out_part

    @pl.when(image == pl.num_programs(0) - 1)
    def _():
        small = total_ref.shape[1] - 4 * width
        column = lax.broadcasted_iota(jnp.int32, (8, small), 1)
        pick = jnp.where(column == experts + lax.broadcasted_iota(jnp.int32, (8, small), 0), 1.0, 0.0)
        total_ref[:, 4 * width :] = dot_first(sums_ref[...].astype(bf16), pick.astype(bf16))
        own = lax.broadcasted_iota(jnp.int32, (1, LANES), 1) < experts
        total_ref[:, 4 * width : 4 * width + LANES] += jnp.where(own, router_ref[...], 0.0)
        half = total_ref.shape[1] // 2

        @pl.when(core_ref[0] == 0)
        def _():
            mine_ref[...] = total_ref[:, :half].astype(bf16)
            other_ref[...] = total_ref[:, half:].astype(bf16)

        @pl.when(core_ref[0] != 0)
        def _():
            other_ref[...] = total_ref[:, :half].astype(bf16)
            mine_ref[...] = total_ref[:, half:].astype(bf16)


def attention_backward(
    core, image_slots, x, cot, middle, qkv, packed, vec, h1, attended, router_grad, back, experts, seq_len
):
    images, rows, width = x.shape
    columns = 4 * width + round_up(experts + VECTORS, 2 * LANES)

    def spec(columns):
        return pl.BlockSpec((1, rows, columns), lambda i: (i, 0, 0))

    half = jax.ShapeDtypeStruct((width, columns // 2), bf16)
    return pl.pallas_call(
        functools.partial(backward_kernel, seq_len, width, experts, len(back)),
        grid=(images,),
        in_specs=[
            scalar_spec(),
            pl.BlockSpec((1, *image_slots.shape[1:]), lambda i: (i, 0, 0)),
            spec(width),
            spec(width),
            spec(width),
            spec(3 * width),
            whole(packed.shape),
            whole(vec.shape),
            spec(width),
            spec(width),
            whole(router_grad.shape),
        ]
        + [whole(part.shape) for part in back],
        out_specs=[spec(width), whole(half.shape), whole(half.shape)],
        out_shape=[jax.ShapeDtypeStruct(x.shape, bf16), half, half],
        scratch_shapes=[
            pltpu.VMEM((rows, 3 * width), bf16),
            pltpu.VMEM((8, width), f32),
            pltpu.VMEM((width, columns), f32),
        ],
        compiler_params=params(1),
        cost_estimate=cost(),
        name="attention_backward",
    )(core, image_slots, x, cot, middle, qkv, packed, vec, h1, attended, router_grad, *back)


def swap(value, axis, distance):
    count = lax.axis_size(axis)
    return lax.ppermute(value, axis, [(i, i ^ distance) for i in range(count)])


def exchange(rows):
    experts = lax.axis_size("shard")
    blocks = rows.reshape(experts, rows.shape[0] // experts, rows.shape[1])
    moved = lax.all_to_all(blocks, "shard", split_axis=0, concat_axis=0, tiled=True)
    return moved.reshape(rows.shape)


def add(left, right):
    return (left.astype(f32) + right.astype(f32)).astype(bf16)


def halves(value, core, axis):
    half = value.shape[axis] // 2
    mine = lax.dynamic_slice_in_dim(value, core * half, half, axis)
    other = lax.dynamic_slice_in_dim(value, (1 - core) * half, half, axis)
    return mine, other


def join(mine, theirs, core, axis):
    first = jnp.where(core == 0, mine, theirs)
    second = jnp.where(core == 0, theirs, mine)
    return jnp.concatenate([first, second], axis)


def over_chips(value):
    step = 2
    while step < lax.axis_size("replica"):
        value = add(value, swap(value, "replica", step))
        step *= 2
    return value


def tie(*values):
    return lax.optimization_barrier(values)


def per_device(
    images,
    routes,
    cotangent,
    ln1_gain,
    ln1_bias,
    qkv_weight,
    q_bias,
    v_bias,
    out_weight,
    out_bias,
    ln2_gain,
    ln2_bias,
    router_weight,
    expert_in,
    expert_in_bias,
    expert_out,
    expert_out_bias,
):
    experts = lax.axis_size("shard")
    here = lax.axis_index("shard").reshape(1).astype(jnp.int32)
    core = lax.axis_index("replica") % 2
    images_here, seq_len, width = images.shape
    tokens_here = images_here * seq_len
    capacity = 14 * tokens_here // (5 * experts)
    first_part = round_up(-(-capacity // 2), 16)
    parts = [(0, first_part), (first_part, round_up(capacity - first_part, 8))]
    rows = round_up(seq_len, 16)
    tokens = images_here * rows

    columns = [ln1_gain, ln1_bias, q_bias, v_bias, out_bias, ln2_gain, ln2_bias]
    small = jnp.concatenate([router_weight, jnp.stack(columns, 1)], 1)
    small_width = round_up(small.shape[1], LANES)
    small = jnp.pad(small, ((0, 0), (0, small_width - small.shape[1])))
    shard = jnp.concatenate([qkv_weight, out_weight, small], 1)
    mine, _ = halves(shard, core, 0)
    mine = lax.all_gather(mine, "shard", axis=0, tiled=False)

    pad_rows = ((0, 0), (0, rows - seq_len), (0, 0))
    route_rows = jnp.pad(routes, pad_rows, constant_values=-1).reshape(tokens, 2).T
    expert_ids = jnp.arange(experts, dtype=jnp.int32)[:, None]
    named = (route_rows[0:1] == expert_ids) | (route_rows[1:2] == expert_ids)
    token = jnp.arange(tokens, dtype=jnp.int32)
    earlier = (token[:, None] < token[None, :]).astype(bf16)
    ranking = dot(named.astype(bf16), earlier).astype(jnp.int32)
    ranks = [
        jnp.sum(jnp.where(route_rows[j][None] == expert_ids, ranking, 0), 0) for j in range(2)
    ]
    there = route_rows[0] >= 0
    part_slots = [
        jnp.where(
            there & (ranks[j] >= first) & (ranks[j] < first + size),
            route_rows[j] * size + ranks[j] - first,
            -1,
        )
        for first, size in parts
        for j in range(2)
    ]
    part_rows = [jnp.stack(part_slots[2 * i : 2 * i + 2], 0) for i in range(len(parts))]
    image_slots = part_slots + part_slots[:1] * (8 - len(part_slots))
    image_slots = jnp.stack(image_slots, 0).reshape(8, images_here, rows).swapaxes(0, 1)

    def place(values):
        return [
            dispatch(part_rows[i], values, experts * size, 4) for i, (_, size) in enumerate(parts)
        ]

    x = jnp.pad(images, pad_rows)
    cot = jnp.pad(cotangent, pad_rows)
    cot_sent = place(cot.reshape(tokens, width))
    cot_there = [exchange(cot_sent[0])]
    mine, cot_there[0], cot_sent[1], x, cot, image_slots = tie(
        mine, cot_there[0], cot_sent[1], x, cot, image_slots
    )
    cot_there.append(exchange(cot_sent[1]))
    packed = join(mine, swap(mine, "replica", 1), core, 1).reshape(width, shard.shape[1])
    small_full = packed[:, 4 * width :]
    lane = jnp.arange(small_width, dtype=jnp.int32)[None, :]
    router = jnp.where(lane < experts, small_full, jnp.zeros_like(small_full))[:, :LANES]
    pick = (lane == experts + jnp.arange(8, dtype=jnp.int32)[:, None]).astype(bf16)
    vec = dot_last(pick, small_full)

    h1, qkv, attended, middle, h2 = attention_forward(x, packed, vec, seq_len)
    sent = place(h2.reshape(tokens, width))
    sent[0], cot_there[1] = tie(sent[0], cot_there[1])
    arrived = [exchange(sent[0])]
    sent[1], arrived[0] = tie(sent[1], arrived[0])
    arrived.append(exchange(sent[1]))

    weights = (expert_in, expert_in_bias, expert_out, expert_out_bias)
    first = expert_chunk(here, arrived[0], cot_there[0], weights, router, experts)
    back_first, arrived[1] = tie(first[0], arrived[1])
    back = [exchange(back_first)]
    second = expert_chunk(here, arrived[1], cot_there[1], weights, router, experts)
    back_second, back[0], *second = tie(second[0], back[0], *second[1:])
    back.append(exchange(back_second))
    gated, hiddens, inners, outers, logits, in_sums, out_sums = zip(first[1:], second)

    core_here = core.reshape(1).astype(jnp.int32)
    out_mine, out_other = out_grad(core_here, hiddens, outers)
    in_mine, in_other, router_grad = in_grad(core_here, arrived, inners, logits)
    back[1], out_mine, out_other, in_mine, in_other = tie(
        back[1], out_mine, out_other, in_mine, in_other
    )
    out_mine = add(out_mine, swap(out_other, "replica", 1))
    in_mine = add(in_mine, swap(in_other, "replica", 1))
    biases = jnp.concatenate([sum(in_sums)[0], sum(out_sums)[0]]).reshape(-1, width).astype(bf16)
    biases = over_chips(add(biases, swap(biases, "replica", 1)))
    out_mine = over_chips(out_mine)
    in_mine, out_mine = tie(in_mine, out_mine)
    in_mine = over_chips(in_mine)

    first_gated, back[1] = tie(gated[0], back[1])
    returned = [exchange(first_gated)]
    input_grad, mine, other = attention_backward(
        core_here,
        image_slots,
        x,
        cot,
        middle,
        qkv,
        packed,
        vec,
        h1,
        attended,
        router_grad,
        back,
        experts,
        seq_len,
    )
    mine, other, returned[0] = tie(mine, other, returned[0])
    mine = add(mine, swap(other, "replica", 1))
    mine, out_mine = tie(mine, out_mine)
    pieces = exchange(mine)
    second_gated, pieces = tie(gated[1], pieces)
    returned.append(exchange(second_gated))
    pieces = pieces.reshape(experts, width // experts, -1)
    mine = jnp.sum(pieces.astype(f32), 0).astype(bf16)
    mine = over_chips(mine)
    summed = join(mine, swap(mine, "replica", 1), core, 1).astype(f32)

    output = combine_output(image_slots, middle, returned)
    expert_out_grad = widen(core_here, out_mine, swap(out_mine, "replica", 1))[None]
    expert_in_grad = widen(core_here, in_mine, swap(in_mine, "replica", 1))[None]
    biases = biases.astype(f32).reshape(1, -1)
    hidden_width = expert_in_bias.shape[1]
    small_sum = summed[:, 4 * width :]
    vector_sums = small_sum[:, experts : experts + VECTORS].T
    return (
        output[:, :seq_len],
        input_grad[:, :seq_len],
        vector_sums[GAIN_ONE],
        vector_sums[SHIFT_ONE],
        summed[:, : 3 * width],
        vector_sums[QUERY_BIAS],
        vector_sums[VALUE_BIAS],
        summed[:, 3 * width : 4 * width],
        vector_sums[OUT_SHIFT],
        vector_sums[GAIN_TWO],
        vector_sums[SHIFT_TWO],
        small_sum[:, :experts],
        expert_in_grad,
        biases[:, :hidden_width],
        expert_out_grad,
        biases[:, hidden_width:],
    )


def solution(mesh):
    return jax.shard_map(
        per_device,
        mesh=mesh,
        in_specs=(
            P(("replica", "shard"), None, None),
            P(("replica", "shard"), None, None),
            P(("replica", "shard"), None, None),
            P("shard"),
            P("shard"),
            P("shard", None),
            P("shard"),
            P("shard"),
            P("shard", None),
            P("shard"),
            P("shard"),
            P("shard"),
            P("shard", None),
            P("shard", None, None),
            P("shard", None),
            P("shard", None, None),
            P("shard", None),
        ),
        out_specs=(
            P(("replica", "shard"), None, None),
            P(("replica", "shard"), None, None),
            P("shard"),
            P("shard"),
            P("shard", None),
            P("shard"),
            P("shard"),
            P("shard", None),
            P("shard"),
            P("shard"),
            P("shard"),
            P("shard", None),
            P("shard", None, None),
            P("shard", None),
            P("shard", None, None),
            P("shard", None),
        ),
        check_vma=False,
    )
```

```python
import functools

import jax
import jax.numpy as jnp
from jax import lax
from jax.experimental import pallas as pl
from jax.experimental.pallas import tpu as pltpu
from jax.sharding import PartitionSpec as P

HEADS = 12
HEAD_DIM = 64
LANES = 128
VMEM_BYTES = 56 * 1024 * 1024


eps_norm = 1e-06
f32 = jnp.float32
bf16 = jnp.bfloat16

GAIN_ONE, SHIFT_ONE, QUERY_BIAS, VALUE_BIAS, OUT_SHIFT, GAIN_TWO, SHIFT_TWO = range(7)
VECTORS = 7


def round_up(value, multiple):
    return -(-value // multiple) * multiple


def normalize(values):
    average = jnp.mean(values, -1, keepdims=True)
    centred = values - average
    variance = jnp.mean(centred * centred, -1, keepdims=True)
    inverse = lax.rsqrt(variance + eps_norm)
    return (centred * inverse, inverse)


def norm_back(grad_out, scaled, inverse, gain_vec):
    gain_grad = jnp.sum(grad_out * scaled, 0, keepdims=True)
    shift_grad = jnp.sum(grad_out, 0, keepdims=True)
    grad_scaled = grad_out * gain_vec
    first_term = jnp.mean(grad_scaled, -1, keepdims=True)
    second_term = jnp.mean(grad_scaled * scaled, -1, keepdims=True)
    return (inverse * (grad_scaled - first_term - scaled * second_term), gain_grad, shift_grad)


def dot(left, right):
    return jnp.dot(left, right, preferred_element_type=f32)


def dot_last(left, right):
    return lax.dot_general(left, right, (((1,), (1,)), ((), ())), preferred_element_type=f32)


def dot_first(left, right):
    return lax.dot_general(left, right, (((0,), (0,)), ((), ())), preferred_element_type=f32)


def params(steps=0):
    return pltpu.CompilerParams(
        vmem_limit_bytes=VMEM_BYTES,
        dimension_semantics=("arbitrary",) * steps if steps else None,
    )


def cost():
    return pl.CostEstimate(flops=1 << 20, bytes_accessed=1 << 16, transcendentals=0)


def whole(shape):
    return pl.BlockSpec(shape, lambda *_: (0,) * len(shape))


def scalar_spec():
    return pl.BlockSpec(memory_space=pltpu.SMEM)


def forward_kernel(seq_len, width, x_ref, w_ref, vec_ref, h1_ref, qkv_ref, o_ref, mid_ref, h2_ref):
    vec = vec_ref[...]

    def row(index):
        return vec[index : index + 1]

    x = x_ref[0].astype(f32)
    scaled, _ = normalize(x)
    h1 = (scaled * row(GAIN_ONE) + row(SHIFT_ONE)).astype(bf16)
    h1_ref[0] = h1
    for part, bias in ((0, QUERY_BIAS), (1, None), (2, VALUE_BIAS)):
        block = dot(h1, w_ref[:, part * width : (part + 1) * width])
        if bias is not None:
            block = block + row(bias)
        qkv_ref[0, :, part * width : (part + 1) * width] = block.astype(bf16)
    rows = x.shape[0]
    lane = lax.broadcasted_iota(jnp.int32, (1, LANES), 1)
    key_there = lax.broadcasted_iota(jnp.int32, (1, rows), 1) < seq_len
    factor = HEAD_DIM ** (-0.5)
    for pair in range(width // LANES):
        at = pair * LANES
        queries = qkv_ref[0, :, at : at + LANES] * jnp.asarray(factor, bf16)
        keys = qkv_ref[0, :, width + at : width + at + LANES]
        values = qkv_ref[0, :, 2 * width + at : 2 * width + at + LANES]
        total = None
        for half in range(LANES // HEAD_DIM):
            mine = (lane // HEAD_DIM) == half
            scores = dot_last(jnp.where(mine, queries, jnp.zeros_like(queries)), keys)
            scores = jnp.where(key_there, scores, -1e30)
            powers = jnp.exp(scores - jnp.max(scores, -1, keepdims=True))
            probs = (powers * (1.0 / jnp.sum(powers, -1, keepdims=True))).astype(bf16)
            part = dot(probs, jnp.where(mine, values, jnp.zeros_like(values)))
            total = part if total is None else total + part
        o_ref[0, :, at : at + LANES] = total.astype(bf16)
    middle = x + (dot(o_ref[0], w_ref[:, 3 * width : 4 * width]) + row(OUT_SHIFT))
    mid_ref[0] = middle
    scaled, _ = normalize(middle)
    h2_ref[0] = (scaled * row(GAIN_TWO) + row(SHIFT_TWO)).astype(bf16)


def attention_forward(x, packed, vec, seq_len):
    images, rows, width = x.shape

    def spec(columns):
        return pl.BlockSpec((1, rows, columns), lambda i: (i, 0, 0))

    def shape(columns, dtype):
        return jax.ShapeDtypeStruct((images, rows, columns), dtype)

    return pl.pallas_call(
        functools.partial(forward_kernel, seq_len, width),
        grid=(images,),
        in_specs=[spec(width), whole(packed.shape), whole(vec.shape)],
        out_specs=[spec(width), spec(3 * width), spec(width), spec(width), spec(width)],
        out_shape=[
            shape(width, bf16),
            shape(3 * width, bf16),
            shape(width, bf16),
            shape(width, f32),
            shape(width, bf16),
        ],
        compiler_params=params(1),
        cost_estimate=cost(),
        name="attention_forward",
    )(x, packed, vec)


def dispatch_kernel(slot_ref, rows_ref, out_ref):
    slots = slot_ref[...]
    high = out_ref.shape[0]
    slot = lax.broadcasted_iota(jnp.int32, (high, rows_ref.shape[0]), 0) + pl.program_id(0) * high
    hot = jnp.where((slot == slots[0:1]) | (slot == slots[1:2]), 1.0, 0.0).astype(bf16)
    out_ref[...] = dot(hot, rows_ref[...]).astype(bf16)


def dispatch(slots, rows, places, steps):
    width = rows.shape[1]
    return pl.pallas_call(
        dispatch_kernel,
        in_specs=[whole(slots.shape), whole(rows.shape)],
        out_specs=pl.BlockSpec((places // steps, width), lambda e: (e, 0)),
        grid=(steps,),
        out_shape=jax.ShapeDtypeStruct((places, width), bf16),
        compiler_params=params(1),
        cost_estimate=cost(),
        name="dispatch",
    )(slots, rows)


def expert_kernel(
    experts,
    tiles,
    here_ref,
    rows_ref,
    cot_ref,
    in_ref,
    in_bias_ref,
    out_ref,
    out_bias_ref,
    router_ref,
    back_ref,
    gated_ref,
    hidden_ref,
    inner_ref,
    outer_ref,
    logit_ref,
    in_sum_ref,
    out_sum_ref,
    slope_ref,
    total_ref,
):
    phase, tile = pl.program_id(0), pl.program_id(1)
    high = rows_ref.shape[0] // 4
    blocks = [slice(i * high, (i + 1) * high) for i in range(4)]

    @pl.when(phase == 0)
    def _():
        slant = 0.7978845608028654
        for block in blocks:
            act = dot(rows_ref[block, :], in_ref[0]) + in_bias_ref[...].astype(f32)
            square = act * act
            bend = jnp.tanh(act * (slant + (slant * 0.044715) * square))
            half = 0.5 + 0.5 * bend
            hidden_ref[block, :] = (act * half).astype(bf16)
            slope_ref[tile, block, :] = half + (0.5 * act) * (1.0 - bend * bend) * (
                slant + (3.0 * slant * 0.044715) * square
            )
        part = dot(hidden_ref[...], out_ref[0])

        @pl.when(tile == 0)
        def _():
            total_ref[...] = part

        @pl.when(tile > 0)
        def _():
            total_ref[...] += part

    @pl.when((phase == 0) & (tile == tiles - 1))
    def _():
        outer = total_ref[...] + out_bias_ref[...].astype(f32)
        logits = dot(rows_ref[...], router_ref[...])
        lane = lax.broadcasted_iota(jnp.int32, (1, LANES), 1)
        logits = jnp.where(lane < experts, logits, -1e30)
        powers = jnp.exp(logits - jnp.max(logits, -1, keepdims=True))
        probs = powers / jnp.sum(powers, -1, keepdims=True)
        is_here = jnp.where(lane == here_ref[0], 1.0, 0.0)
        gate = jnp.sum(probs * is_here, -1, keepdims=True)
        gated_ref[...] = (gate * outer).astype(bf16)
        cot = cot_ref[...].astype(f32)
        gate_grad = jnp.sum(cot * outer, -1, keepdims=True)
        outer_grad = (gate * cot).astype(bf16)
        outer_ref[...] = outer_grad
        out_sum_ref[...] = jnp.sum(outer_grad.astype(f32), 0, keepdims=True)
        logit_ref[...] = ((gate_grad * gate) * (is_here - probs)).astype(bf16)

    @pl.when(phase == 1)
    def _():
        in_sum = None
        for block in blocks:
            hidden_grad = dot_last(outer_ref[block, :], out_ref[0])
            inner = (hidden_grad * slope_ref[tile, block, :]).astype(bf16)
            inner_ref[block, :] = inner
            block_sum = jnp.sum(inner.astype(f32), 0, keepdims=True)
            in_sum = block_sum if in_sum is None else in_sum + block_sum
        in_sum_ref[...] = in_sum
        part = dot_last(inner_ref[...], in_ref[0])

        @pl.when(tile == 0)
        def _():
            total_ref[...] = part + dot_last(logit_ref[...], router_ref[...])

        @pl.when(tile > 0)
        def _():
            total_ref[...] += part

    @pl.when((phase == 1) & (tile == tiles - 1))
    def _():
        back_ref[...] = total_ref[...].astype(bf16)


def expert_chunk(here, rows_in, cots, weights, router, experts):
    rows, width = rows_in.shape
    weight_in, bias_in, weight_out, bias_out = weights
    hidden = weight_in.shape[2]
    depth = 512
    tiles = hidden // depth

    def first_phase(p, f, _):
        return (0, jnp.where(p == 0, f, tiles - 1))

    def second_phase(p, f, _):
        return (0, jnp.where(p == 0, 0, f))

    every = whole((rows, width))

    def shape(columns):
        return jax.ShapeDtypeStruct((rows, columns), bf16)

    return pl.pallas_call(
        functools.partial(expert_kernel, experts, tiles),
        grid_spec=pltpu.PrefetchScalarGridSpec(
            num_scalar_prefetch=1,
            grid=(2, tiles),
            in_specs=[
                every,
                every,
                pl.BlockSpec((1, width, depth), lambda p, f, _: (0, 0, f)),
                pl.BlockSpec((1, depth), lambda p, f, _: (0, f)),
                pl.BlockSpec((1, depth, width), lambda p, f, _: (0, f, 0)),
                whole((1, width)),
                whole(router.shape),
            ],
            out_specs=[
                every,
                every,
                pl.BlockSpec((rows, depth), first_phase),
                pl.BlockSpec((rows, depth), second_phase),
                every,
                whole((rows, LANES)),
                pl.BlockSpec((1, depth), second_phase),
                whole((1, width)),
            ],
            scratch_shapes=[
                pltpu.VMEM((tiles, rows, depth), f32),
                pltpu.VMEM((rows, width), f32),
            ],
        ),
        out_shape=[
            shape(width),
            shape(width),
            shape(hidden),
            shape(hidden),
            shape(width),
            shape(LANES),
            jax.ShapeDtypeStruct((1, hidden), f32),
            jax.ShapeDtypeStruct((1, width), f32),
        ],
        compiler_params=params(2),
        cost_estimate=cost(),
        name="expert_chunk",
    )(here, rows_in, cots, weight_in, bias_in, weight_out, bias_out, router)


def out_grad_kernel(parts, core_ref, *refs):
    hidden_refs, outer_refs = refs[:parts], refs[parts : 2 * parts]
    mine_ref, other_ref = refs[2 * parts : 2 * parts + 2]
    turned_refs = refs[2 * parts + 2 :]
    step = pl.program_id(0)

    @pl.when(step == 0)
    def _():
        for outer_ref, turned_ref in zip(outer_refs, turned_refs):
            turned_ref[...] = outer_ref[...].T

    total = sum(dot(turned[...], hidden[...]) for turned, hidden in zip(turned_refs, hidden_refs))
    block = total.astype(bf16).T

    @pl.when(step < pl.num_programs(0) // 2)
    def _():
        other_ref[...] = block

    @pl.when(step >= pl.num_programs(0) // 2)
    def _():
        mine_ref[...] = block


def out_grad(core, hiddens, outers):
    parts = len(hiddens)
    high, wide = hiddens[0].shape[1], outers[0].shape[1]
    tile = 512
    half = high // 2 // tile

    def place(i, core_ref):
        own = i >= half
        return (0, jnp.where(own, core_ref[0], 1 - core_ref[0]) * half + i - own * half)

    return pl.pallas_call(
        functools.partial(out_grad_kernel, parts),
        grid_spec=pltpu.PrefetchScalarGridSpec(
            num_scalar_prefetch=1,
            grid=(2 * half,),
            in_specs=[pl.BlockSpec((rows.shape[0], tile), place) for rows in hiddens]
            + [whole(rows.shape) for rows in outers],
            out_specs=[
                pl.BlockSpec((tile, wide), lambda i, _: (jnp.maximum(i - half, 0), 0)),
                pl.BlockSpec((tile, wide), lambda i, _: (jnp.minimum(i, half - 1), 0)),
            ],
            scratch_shapes=[pltpu.VMEM((wide, rows.shape[0]), bf16) for rows in outers],
        ),
        out_shape=[jax.ShapeDtypeStruct((high // 2, wide), bf16)] * 2,
        compiler_params=params(1),
        cost_estimate=cost(),
        name="out_grad",
    )(core, *hiddens, *outers)


def in_grad_kernel(parts, core_ref, *refs):
    arrived_refs, inner_refs, logit_refs = (refs[i * parts : (i + 1) * parts] for i in range(3))
    mine_ref, other_ref, router_ref = refs[3 * parts : 3 * parts + 3]
    turned_refs = refs[3 * parts + 3 :]
    half = mine_ref.shape[0]

    @pl.when(pl.program_id(0) == 0)
    def _():
        for arrived_ref, turned_ref in zip(arrived_refs, turned_refs):
            turned = arrived_ref[...].T
            turned_ref[0] = turned[:half]
            turned_ref[1] = turned[half:]
        for h in range(2):
            router_ref[h * half : (h + 1) * half, :] = sum(
                dot(turned[h], logit[...]) for turned, logit in zip(turned_refs, logit_refs)
            )

    core = core_ref[0]
    mine_ref[...] = sum(
        dot(turned[core], inner[...]) for turned, inner in zip(turned_refs, inner_refs)
    ).astype(bf16)
    other_ref[...] = sum(
        dot(turned[1 - core], inner[...]) for turned, inner in zip(turned_refs, inner_refs)
    ).astype(bf16)


def in_grad(core, arrived, inners, logits):
    parts = len(inners)
    high, wide = arrived[0].shape[1], inners[0].shape[1]
    tile = 512
    spec = pl.BlockSpec((high // 2, tile), lambda i, _: (0, i))
    return pl.pallas_call(
        functools.partial(in_grad_kernel, parts),
        grid_spec=pltpu.PrefetchScalarGridSpec(
            num_scalar_prefetch=1,
            grid=(wide // tile,),
            in_specs=[whole(rows.shape) for rows in arrived]
            + [pl.BlockSpec((rows.shape[0], tile), lambda i, _: (0, i)) for rows in inners]
            + [whole(rows.shape) for rows in logits],
            out_specs=[spec, spec, whole((high, LANES))],
            scratch_shapes=[pltpu.VMEM((2, high // 2, rows.shape[0]), bf16) for rows in arrived],
        ),
        out_shape=[jax.ShapeDtypeStruct((high // 2, wide), bf16)] * 2
        + [jax.ShapeDtypeStruct((high, LANES), f32)],
        compiler_params=params(1),
        cost_estimate=cost(),
        name="in_grad",
    )(core, *arrived, *inners, *logits)


def widen_kernel(core_ref, mine_ref, theirs_ref, out_ref):
    own = pl.program_id(0) == core_ref[0]

    @pl.when(own)
    def _():
        out_ref[...] = mine_ref[...].astype(f32)

    @pl.when(jnp.logical_not(own))
    def _():
        out_ref[...] = theirs_ref[...].astype(f32)


def widen(core, mine, theirs):
    high, wide = mine.shape
    tile = high // 4

    def block(is_mine):
        def index(h, i, core_ref):
            used = (h == core_ref[0]) == is_mine
            return (jnp.where(used, i, 0), 0)

        return pl.BlockSpec((tile, wide), index)

    return pl.pallas_call(
        widen_kernel,
        grid_spec=pltpu.PrefetchScalarGridSpec(
            num_scalar_prefetch=1,
            grid=(2, 4),
            in_specs=[block(True), block(False)],
            out_specs=pl.BlockSpec((tile, wide), lambda h, i, _: (h * 4 + i, 0)),
        ),
        out_shape=jax.ShapeDtypeStruct((2 * high, wide), f32),
        compiler_params=params(2),
        cost_estimate=cost(),
        name="widen",
    )(core, mine, theirs)


def collect(slots, rows):
    slot = lax.broadcasted_iota(jnp.int32, (1, rows.shape[0]), 1)
    hot = (slots[:, 0:1] == slot) | (slots[:, 1:2] == slot)
    return dot(jnp.where(hot, 1.0, 0.0).astype(bf16), rows)


def collect_parts(slots, part_refs):
    return sum(
        collect(slots[:, 2 * part : 2 * part + 2], part_ref[...])
        for part, part_ref in enumerate(part_refs)
    )


def output_kernel(slot_ref, mid_ref, *refs):
    refs[-1][0] = (mid_ref[0] + collect_parts(slot_ref[0].T, refs[:-1])).astype(bf16)


def combine_output(image_slots, middle, returned):
    images, rows, width = middle.shape
    spec = pl.BlockSpec((1, rows, width), lambda i: (i, 0, 0))
    return pl.pallas_call(
        output_kernel,
        grid=(images,),
        in_specs=[pl.BlockSpec((1, *image_slots.shape[1:]), lambda i: (i, 0, 0)), spec]
        + [whole(part.shape) for part in returned],
        out_specs=spec,
        out_shape=jax.ShapeDtypeStruct((images, rows, width), bf16),
        compiler_params=params(1),
        cost_estimate=cost(),
        name="combine_output",
    )(image_slots, middle, *returned)


def backward_kernel(seq_len, width, experts, parts, core_ref, *refs):
    slot_ref, x_ref, cot_ref, mid_ref, qkv_ref, w_ref, vec_ref = refs[:7]
    h1_ref, o_ref, router_ref = refs[7:10]
    part_refs = refs[10 : 10 + parts]
    grad_ref, mine_ref, other_ref, dqkv_ref, sums_ref, total_ref = refs[10 + parts :]
    vec = vec_ref[...]

    def row(index):
        return vec[index : index + 1]

    h2_grad = collect_parts(slot_ref[0].T, part_refs)
    scaled, inverse = normalize(mid_ref[0])
    norm_grad, gain_two_grad, shift_two_grad = norm_back(h2_grad, scaled, inverse, row(GAIN_TWO))
    mid_grad = cot_ref[0].astype(f32) + norm_grad
    branch = mid_grad.astype(bf16)
    out_shift_grad = jnp.sum(branch.astype(f32), 0, keepdims=True)
    o_grad = dot_last(branch, w_ref[:, 3 * width : 4 * width]).astype(bf16)

    rows = branch.shape[0]
    lane = lax.broadcasted_iota(jnp.int32, (1, LANES), 1)
    key_there = lax.broadcasted_iota(jnp.int32, (rows, 1), 0) < seq_len
    factor = HEAD_DIM ** (-0.5)
    for pair in range(width // LANES):
        at = pair * LANES
        queries = qkv_ref[0, :, at : at + LANES] * jnp.asarray(factor, bf16)
        keys = qkv_ref[0, :, width + at : width + at + LANES]
        values = qkv_ref[0, :, 2 * width + at : 2 * width + at + LANES]
        grads = o_grad[:, at : at + LANES]
        query_grad = key_grad = value_grad = None
        for half in range(LANES // HEAD_DIM):
            mine = (lane // HEAD_DIM) == half

            def only(slab):
                return jnp.where(mine, slab, jnp.zeros_like(slab))

            own_queries, own_keys, own_grads = only(queries), only(keys), only(grads)
            scores = dot_last(own_keys, queries)
            scores = jnp.where(key_there, scores, -1e30)
            powers = jnp.exp(scores - jnp.max(scores, 0, keepdims=True))
            probs = powers * (1.0 / jnp.sum(powers, 0, keepdims=True))
            prob_grad = dot_last(values, own_grads)
            spread = jnp.sum(probs * prob_grad, 0, keepdims=True)
            score_grad = (probs * (prob_grad - spread)).astype(bf16)
            value_part = dot(probs.astype(bf16), own_grads)
            key_part = dot(score_grad, own_queries)
            query_part = dot_first(score_grad, own_keys)
            if half == 0:
                query_grad, key_grad, value_grad = query_part, key_part, value_part
            else:
                query_grad += query_part
                key_grad += key_part
                value_grad += value_part
        dqkv_ref[:, at : at + LANES] = (query_grad * factor).astype(bf16)
        dqkv_ref[:, width + at : width + at + LANES] = key_grad.astype(bf16)
        dqkv_ref[:, 2 * width + at : 2 * width + at + LANES] = value_grad.astype(bf16)

    h1_grad = dot_last(dqkv_ref[...], w_ref[:, : 3 * width])
    query_sum = jnp.sum(dqkv_ref[:, :width].astype(f32), 0, keepdims=True)
    value_sum = jnp.sum(dqkv_ref[:, 2 * width :].astype(f32), 0, keepdims=True)
    scaled, inverse = normalize(x_ref[0].astype(f32))
    norm_grad, gain_one_grad, shift_one_grad = norm_back(h1_grad, scaled, inverse, row(GAIN_ONE))
    grad_ref[0] = (mid_grad + norm_grad).astype(bf16)
    sums = [
        gain_one_grad,
        shift_one_grad,
        query_sum,
        value_sum,
        out_shift_grad,
        gain_two_grad,
        shift_two_grad,
        jnp.zeros((sums_ref.shape[0] - VECTORS, width), f32),
    ]
    sums = jnp.concatenate(sums, 0)

    image = pl.program_id(0)
    qkv_part = dot_first(h1_ref[0], dqkv_ref[...])
    out_part = dot_first(o_ref[0], branch)

    @pl.when(image == 0)
    def _():
        sums_ref[...] = sums
        total_ref[:, : 3 * width] = qkv_part
        total_ref[:, 3 * width : 4 * width] = out_part

    @pl.when(image > 0)
    def _():
        sums_ref[...] += sums
        total_ref[:, : 3 * width] += qkv_part
        total_ref[:, 3 * width : 4 * width] += out_part

    @pl.when(image == pl.num_programs(0) - 1)
    def _():
        small = total_ref.shape[1] - 4 * width
        column = lax.broadcasted_iota(jnp.int32, (8, small), 1)
        pick = jnp.where(column == experts + lax.broadcasted_iota(jnp.int32, (8, small), 0), 1.0, 0.0)
        total_ref[:, 4 * width :] = dot_first(sums_ref[...].astype(bf16), pick.astype(bf16))
        own = lax.broadcasted_iota(jnp.int32, (1, LANES), 1) < experts
        total_ref[:, 4 * width : 4 * width + LANES] += jnp.where(own, router_ref[...], 0.0)
        half = total_ref.shape[1] // 2

        @pl.when(core_ref[0] == 0)
        def _():
            mine_ref[...] = total_ref[:, :half].astype(bf16)
            other_ref[...] = total_ref[:, half:].astype(bf16)

        @pl.when(core_ref[0] != 0)
        def _():
            other_ref[...] = total_ref[:, :half].astype(bf16)
            mine_ref[...] = total_ref[:, half:].astype(bf16)


def attention_backward(
    core, image_slots, x, cot, middle, qkv, packed, vec, h1, attended, router_grad, back, experts, seq_len
):
    images, rows, width = x.shape
    columns = 4 * width + round_up(experts + VECTORS, 2 * LANES)

    def spec(columns):
        return pl.BlockSpec((1, rows, columns), lambda i: (i, 0, 0))

    half = jax.ShapeDtypeStruct((width, columns // 2), bf16)
    return pl.pallas_call(
        functools.partial(backward_kernel, seq_len, width, experts, len(back)),
        grid=(images,),
        in_specs=[
            scalar_spec(),
            pl.BlockSpec((1, *image_slots.shape[1:]), lambda i: (i, 0, 0)),
            spec(width),
            spec(width),
            spec(width),
            spec(3 * width),
            whole(packed.shape),
            whole(vec.shape),
            spec(width),
            spec(width),
            whole(router_grad.shape),
        ]
        + [whole(part.shape) for part in back],
        out_specs=[spec(width), whole(half.shape), whole(half.shape)],
        out_shape=[jax.ShapeDtypeStruct(x.shape, bf16), half, half],
        scratch_shapes=[
            pltpu.VMEM((rows, 3 * width), bf16),
            pltpu.VMEM((8, width), f32),
            pltpu.VMEM((width, columns), f32),
        ],
        compiler_params=params(1),
        cost_estimate=cost(),
        name="attention_backward",
    )(core, image_slots, x, cot, middle, qkv, packed, vec, h1, attended, router_grad, *back)


def swap(value, axis, distance):
    count = lax.axis_size(axis)
    return lax.ppermute(value, axis, [(i, i ^ distance) for i in range(count)])


def exchange(rows):
    experts = lax.axis_size("shard")
    blocks = rows.reshape(experts, rows.shape[0] // experts, rows.shape[1])
    moved = lax.all_to_all(blocks, "shard", split_axis=0, concat_axis=0, tiled=True)
    return moved.reshape(rows.shape)


def add(left, right):
    return (left.astype(f32) + right.astype(f32)).astype(bf16)


def halves(value, core, axis):
    half = value.shape[axis] // 2
    mine = lax.dynamic_slice_in_dim(value, core * half, half, axis)
    other = lax.dynamic_slice_in_dim(value, (1 - core) * half, half, axis)
    return mine, other


def join(mine, theirs, core, axis):
    first = jnp.where(core == 0, mine, theirs)
    second = jnp.where(core == 0, theirs, mine)
    return jnp.concatenate([first, second], axis)


def over_chips(value, step=2):
    while step < lax.axis_size("replica"):
        value = add(value, swap(value, "replica", step))
        step *= 2
    return value


def tie(*values):
    return lax.optimization_barrier(values)


def per_device(
    images,
    routes,
    cotangent,
    ln1_gain,
    ln1_bias,
    qkv_weight,
    q_bias,
    v_bias,
    out_weight,
    out_bias,
    ln2_gain,
    ln2_bias,
    router_weight,
    expert_in,
    expert_in_bias,
    expert_out,
    expert_out_bias,
):
    experts = lax.axis_size("shard")
    here = lax.axis_index("shard").reshape(1).astype(jnp.int32)
    core = lax.axis_index("replica") % 2
    images_here, seq_len, width = images.shape
    tokens_here = images_here * seq_len
    capacity = 14 * tokens_here // (5 * experts)
    first_part = round_up(-(-capacity // 2), 16)
    parts = [(0, first_part), (first_part, round_up(capacity - first_part, 8))]
    rows = round_up(seq_len, 16)
    tokens = images_here * rows

    columns = [ln1_gain, ln1_bias, q_bias, v_bias, out_bias, ln2_gain, ln2_bias]
    small = jnp.concatenate([router_weight, jnp.stack(columns, 1)], 1)
    small_width = round_up(small.shape[1], LANES)
    small = jnp.pad(small, ((0, 0), (0, small_width - small.shape[1])))
    shard = jnp.concatenate([qkv_weight, out_weight, small], 1)
    mine, _ = halves(shard, core, 0)
    mine = lax.all_gather(mine, "shard", axis=0, tiled=False)

    pad_rows = ((0, 0), (0, rows - seq_len), (0, 0))
    route_rows = jnp.pad(routes, pad_rows, constant_values=-1).reshape(tokens, 2).T
    expert_ids = jnp.arange(experts, dtype=jnp.int32)[:, None]
    named = (route_rows[0:1] == expert_ids) | (route_rows[1:2] == expert_ids)
    token = jnp.arange(tokens, dtype=jnp.int32)
    earlier = (token[:, None] < token[None, :]).astype(bf16)
    ranking = dot(named.astype(bf16), earlier).astype(jnp.int32)
    ranks = [
        jnp.sum(jnp.where(route_rows[j][None] == expert_ids, ranking, 0), 0) for j in range(2)
    ]
    there = route_rows[0] >= 0
    part_slots = [
        jnp.where(
            there & (ranks[j] >= first) & (ranks[j] < first + size),
            route_rows[j] * size + ranks[j] - first,
            -1,
        )
        for first, size in parts
        for j in range(2)
    ]
    part_rows = [jnp.stack(part_slots[2 * i : 2 * i + 2], 0) for i in range(len(parts))]
    image_slots = part_slots + part_slots[:1] * (8 - len(part_slots))
    image_slots = jnp.stack(image_slots, 0).reshape(8, images_here, rows).swapaxes(0, 1)

    def place(values):
        return [
            dispatch(part_rows[i], values, experts * size, 4) for i, (_, size) in enumerate(parts)
        ]

    x = jnp.pad(images, pad_rows)
    cot = jnp.pad(cotangent, pad_rows)
    cot_sent = place(cot.reshape(tokens, width))
    cot_there = [exchange(cot_sent[0])]
    mine, cot_there[0], cot_sent[1], x, cot, image_slots = tie(
        mine, cot_there[0], cot_sent[1], x, cot, image_slots
    )
    cot_there.append(exchange(cot_sent[1]))
    packed = join(mine, swap(mine, "replica", 1), core, 1).reshape(width, shard.shape[1])
    small_full = packed[:, 4 * width :]
    lane = jnp.arange(small_width, dtype=jnp.int32)[None, :]
    router = jnp.where(lane < experts, small_full, jnp.zeros_like(small_full))[:, :LANES]
    pick = (lane == experts + jnp.arange(8, dtype=jnp.int32)[:, None]).astype(bf16)
    vec = dot_last(pick, small_full)

    h1, qkv, attended, middle, h2 = attention_forward(x, packed, vec, seq_len)
    sent = place(h2.reshape(tokens, width))
    sent[0], cot_there[1] = tie(sent[0], cot_there[1])
    arrived = [exchange(sent[0])]
    sent[1], arrived[0] = tie(sent[1], arrived[0])
    arrived.append(exchange(sent[1]))

    weights = (expert_in, expert_in_bias, expert_out, expert_out_bias)
    first = expert_chunk(here, arrived[0], cot_there[0], weights, router, experts)
    back_first, arrived[1] = tie(first[0], arrived[1])
    back = [exchange(back_first)]
    second = expert_chunk(here, arrived[1], cot_there[1], weights, router, experts)
    back_second, back[0], *second = tie(second[0], back[0], *second[1:])
    back.append(exchange(back_second))
    gated, hiddens, inners, outers, logits, in_sums, out_sums = zip(first[1:], second)

    core_here = core.reshape(1).astype(jnp.int32)
    out_mine, out_other = out_grad(core_here, hiddens, outers)
    in_mine, in_other, router_grad = in_grad(core_here, arrived, inners, logits)
    back[1], out_mine, out_other, in_mine, in_other = tie(
        back[1], out_mine, out_other, in_mine, in_other
    )
    out_mine = add(out_mine, swap(out_other, "replica", 1))
    in_mine = add(in_mine, swap(in_other, "replica", 1))
    biases = jnp.concatenate([sum(in_sums)[0], sum(out_sums)[0]]).reshape(-1, width).astype(bf16)
    biases = over_chips(add(biases, swap(biases, "replica", 1)))
    out_theirs = swap(out_mine, "replica", 2)

    first_gated, back[1] = tie(gated[0], back[1])
    returned = [exchange(first_gated)]
    input_grad, mine, other = attention_backward(
        core_here,
        image_slots,
        x,
        cot,
        middle,
        qkv,
        packed,
        vec,
        h1,
        attended,
        router_grad,
        back,
        experts,
        seq_len,
    )
    mine, other, returned[0], out_theirs = tie(mine, other, returned[0], out_theirs)
    second_gated, returned[0] = tie(gated[1], returned[0])
    returned.append(exchange(second_gated))
    mine = add(mine, swap(other, "replica", 1)).reshape(experts, width // experts, -1)
    chip = lax.axis_index("replica") // 2 % 2
    mine, other = halves(mine, chip, 1)
    mine = add(mine, swap(other, "replica", 2))
    out_mine = over_chips(add(out_mine, out_theirs), 4)
    in_mine, mine = tie(in_mine, mine)
    in_mine = over_chips(in_mine)
    mine, returned[1] = tie(mine, returned[1])
    pieces = lax.all_to_all(mine, "shard", split_axis=0, concat_axis=0, tiled=True)
    output = combine_output(image_slots, middle, returned)
    expert_out_grad = widen(core_here, out_mine, swap(out_mine, "replica", 1))[None]
    pieces, output, expert_out_grad = tie(pieces, output, expert_out_grad)
    mine = jnp.sum(pieces.astype(f32), 0).astype(bf16)
    mine = over_chips(mine, 4)
    mine = join(mine, swap(mine, "replica", 2), chip, 0)
    summed = join(mine, swap(mine, "replica", 1), core, 1).astype(f32)

    expert_in_grad = widen(core_here, in_mine, swap(in_mine, "replica", 1))[None]
    biases = biases.astype(f32).reshape(1, -1)
    hidden_width = expert_in_bias.shape[1]
    small_sum = summed[:, 4 * width :]
    vector_sums = small_sum[:, experts : experts + VECTORS].T
    return (
        output[:, :seq_len],
        input_grad[:, :seq_len],
        vector_sums[GAIN_ONE],
        vector_sums[SHIFT_ONE],
        summed[:, : 3 * width],
        vector_sums[QUERY_BIAS],
        vector_sums[VALUE_BIAS],
        summed[:, 3 * width : 4 * width],
        vector_sums[OUT_SHIFT],
        vector_sums[GAIN_TWO],
        vector_sums[SHIFT_TWO],
        small_sum[:, :experts],
        expert_in_grad,
        biases[:, :hidden_width],
        expert_out_grad,
        biases[:, hidden_width:],
    )


def solution(mesh):
    return jax.shard_map(
        per_device,
        mesh=mesh,
        in_specs=(
            P(("replica", "shard"), None, None),
            P(("replica", "shard"), None, None),
            P(("replica", "shard"), None, None),
            P("shard"),
            P("shard"),
            P("shard", None),
            P("shard"),
            P("shard"),
            P("shard", None),
            P("shard"),
            P("shard"),
            P("shard"),
            P("shard", None),
            P("shard", None, None),
            P("shard", None),
            P("shard", None, None),
            P("shard", None),
        ),
        out_specs=(
            P(("replica", "shard"), None, None),
            P(("replica", "shard"), None, None),
            P("shard"),
            P("shard"),
            P("shard", None),
            P("shard"),
            P("shard"),
            P("shard", None),
            P("shard"),
            P("shard"),
            P("shard"),
            P("shard", None),
            P("shard", None, None),
            P("shard", None),
            P("shard", None, None),
            P("shard", None),
        ),
        check_vma=False,
    )
```

```python
import functools

import jax
import jax.numpy as jnp
from jax import lax
from jax.experimental import pallas as pl
from jax.experimental.pallas import tpu as pltpu
from jax.sharding import PartitionSpec as P

HEADS = 12
HEAD_DIM = 64
LANES = 128
VMEM_BYTES = 56 * 1024 * 1024


eps_norm = 1e-06
f32 = jnp.float32
bf16 = jnp.bfloat16

GAIN_ONE, SHIFT_ONE, QUERY_BIAS, VALUE_BIAS, OUT_SHIFT, GAIN_TWO, SHIFT_TWO = range(7)
VECTORS = 7


def round_up(value, multiple):
    return -(-value // multiple) * multiple


def normalize(values):
    average = jnp.mean(values, -1, keepdims=True)
    centred = values - average
    variance = jnp.mean(centred * centred, -1, keepdims=True)
    inverse = lax.rsqrt(variance + eps_norm)
    return (centred * inverse, inverse)


def norm_back(grad_out, scaled, inverse, gain_vec):
    gain_grad = jnp.sum(grad_out * scaled, 0, keepdims=True)
    shift_grad = jnp.sum(grad_out, 0, keepdims=True)
    grad_scaled = grad_out * gain_vec
    first_term = jnp.mean(grad_scaled, -1, keepdims=True)
    second_term = jnp.mean(grad_scaled * scaled, -1, keepdims=True)
    return (inverse * (grad_scaled - first_term - scaled * second_term), gain_grad, shift_grad)


def dot(left, right):
    return jnp.dot(left, right, preferred_element_type=f32)


def dot_last(left, right):
    return lax.dot_general(left, right, (((1,), (1,)), ((), ())), preferred_element_type=f32)


def dot_first(left, right):
    return lax.dot_general(left, right, (((0,), (0,)), ((), ())), preferred_element_type=f32)


def params(steps=0):
    return pltpu.CompilerParams(
        vmem_limit_bytes=VMEM_BYTES,
        dimension_semantics=("arbitrary",) * steps if steps else None,
    )


def cost():
    return pl.CostEstimate(flops=1 << 20, bytes_accessed=1 << 16, transcendentals=0)


def whole(shape):
    return pl.BlockSpec(shape, lambda *_: (0,) * len(shape))


def scalar_spec():
    return pl.BlockSpec(memory_space=pltpu.SMEM)


def forward_kernel(seq_len, width, x_ref, w_ref, vec_ref, h1_ref, qkv_ref, o_ref, mid_ref, h2_ref):
    vec = vec_ref[...]

    def row(index):
        return vec[index : index + 1]

    x = x_ref[0].astype(f32)
    scaled, _ = normalize(x)
    h1 = (scaled * row(GAIN_ONE) + row(SHIFT_ONE)).astype(bf16)
    h1_ref[0] = h1
    for part, bias in ((0, QUERY_BIAS), (1, None), (2, VALUE_BIAS)):
        block = dot(h1, w_ref[:, part * width : (part + 1) * width])
        if bias is not None:
            block = block + row(bias)
        qkv_ref[0, :, part * width : (part + 1) * width] = block.astype(bf16)
    rows = x.shape[0]
    lane = lax.broadcasted_iota(jnp.int32, (1, LANES), 1)
    key_there = lax.broadcasted_iota(jnp.int32, (1, rows), 1) < seq_len
    factor = HEAD_DIM ** (-0.5)
    for pair in range(width // LANES):
        at = pair * LANES
        queries = qkv_ref[0, :, at : at + LANES] * jnp.asarray(factor, bf16)
        keys = qkv_ref[0, :, width + at : width + at + LANES]
        values = qkv_ref[0, :, 2 * width + at : 2 * width + at + LANES]
        total = None
        for half in range(LANES // HEAD_DIM):
            mine = (lane // HEAD_DIM) == half
            scores = dot_last(jnp.where(mine, queries, jnp.zeros_like(queries)), keys)
            scores = jnp.where(key_there, scores, -1e30)
            powers = jnp.exp(scores - jnp.max(scores, -1, keepdims=True))
            probs = (powers * (1.0 / jnp.sum(powers, -1, keepdims=True))).astype(bf16)
            part = dot(probs, jnp.where(mine, values, jnp.zeros_like(values)))
            total = part if total is None else total + part
        o_ref[0, :, at : at + LANES] = total.astype(bf16)
    middle = x + (dot(o_ref[0], w_ref[:, 3 * width : 4 * width]) + row(OUT_SHIFT))
    mid_ref[0] = middle
    scaled, _ = normalize(middle)
    h2_ref[0] = (scaled * row(GAIN_TWO) + row(SHIFT_TWO)).astype(bf16)


def attention_forward(x, packed, vec, seq_len):
    images, rows, width = x.shape

    def spec(columns):
        return pl.BlockSpec((1, rows, columns), lambda i: (i, 0, 0))

    def shape(columns, dtype):
        return jax.ShapeDtypeStruct((images, rows, columns), dtype)

    return pl.pallas_call(
        functools.partial(forward_kernel, seq_len, width),
        grid=(images,),
        in_specs=[spec(width), whole(packed.shape), whole(vec.shape)],
        out_specs=[spec(width), spec(3 * width), spec(width), spec(width), spec(width)],
        out_shape=[
            shape(width, bf16),
            shape(3 * width, bf16),
            shape(width, bf16),
            shape(width, f32),
            shape(width, bf16),
        ],
        compiler_params=params(1),
        cost_estimate=cost(),
        name="attention_forward",
    )(x, packed, vec)


def dispatch_kernel(slot_ref, rows_ref, out_ref):
    slots = slot_ref[...]
    high = out_ref.shape[0]
    slot = lax.broadcasted_iota(jnp.int32, (high, rows_ref.shape[0]), 0) + pl.program_id(0) * high
    hot = jnp.where((slot == slots[0:1]) | (slot == slots[1:2]), 1.0, 0.0).astype(bf16)
    out_ref[...] = dot(hot, rows_ref[...]).astype(bf16)


def dispatch(slots, rows, places, steps):
    width = rows.shape[1]
    return pl.pallas_call(
        dispatch_kernel,
        in_specs=[whole(slots.shape), whole(rows.shape)],
        out_specs=pl.BlockSpec((places // steps, width), lambda e: (e, 0)),
        grid=(steps,),
        out_shape=jax.ShapeDtypeStruct((places, width), bf16),
        compiler_params=params(1),
        cost_estimate=cost(),
        name="dispatch",
    )(slots, rows)


def expert_kernel(
    experts,
    tiles,
    here_ref,
    rows_ref,
    cot_ref,
    in_ref,
    in_bias_ref,
    out_ref,
    out_bias_ref,
    router_ref,
    back_ref,
    gated_ref,
    hidden_ref,
    inner_ref,
    outer_ref,
    logit_ref,
    in_sum_ref,
    out_sum_ref,
    slope_ref,
    total_ref,
):
    phase, tile = pl.program_id(0), pl.program_id(1)
    high = rows_ref.shape[0] // 4
    blocks = [slice(i * high, (i + 1) * high) for i in range(4)]

    @pl.when(phase == 0)
    def _():
        slant = 0.7978845608028654
        for block in blocks:
            act = dot(rows_ref[block, :], in_ref[0]) + in_bias_ref[...].astype(f32)
            square = act * act
            bend = jnp.tanh(act * (slant + (slant * 0.044715) * square))
            half = 0.5 + 0.5 * bend
            hidden_ref[block, :] = (act * half).astype(bf16)
            slope_ref[tile, block, :] = half + (0.5 * act) * (1.0 - bend * bend) * (
                slant + (3.0 * slant * 0.044715) * square
            )
        part = dot(hidden_ref[...], out_ref[0])

        @pl.when(tile == 0)
        def _():
            total_ref[...] = part

        @pl.when(tile > 0)
        def _():
            total_ref[...] += part

    @pl.when((phase == 0) & (tile == tiles - 1))
    def _():
        outer = total_ref[...] + out_bias_ref[...].astype(f32)
        logits = dot(rows_ref[...], router_ref[...])
        lane = lax.broadcasted_iota(jnp.int32, (1, LANES), 1)
        logits = jnp.where(lane < experts, logits, -1e30)
        powers = jnp.exp(logits - jnp.max(logits, -1, keepdims=True))
        probs = powers / jnp.sum(powers, -1, keepdims=True)
        is_here = jnp.where(lane == here_ref[0], 1.0, 0.0)
        gate = jnp.sum(probs * is_here, -1, keepdims=True)
        gated_ref[...] = (gate * outer).astype(bf16)
        cot = cot_ref[...].astype(f32)
        gate_grad = jnp.sum(cot * outer, -1, keepdims=True)
        outer_grad = (gate * cot).astype(bf16)
        outer_ref[...] = outer_grad
        out_sum_ref[...] = jnp.sum(outer_grad.astype(f32), 0, keepdims=True)
        logit_ref[...] = ((gate_grad * gate) * (is_here - probs)).astype(bf16)

    @pl.when(phase == 1)
    def _():
        in_sum = None
        for block in blocks:
            hidden_grad = dot_last(outer_ref[block, :], out_ref[0])
            inner = (hidden_grad * slope_ref[tile, block, :]).astype(bf16)
            inner_ref[block, :] = inner
            block_sum = jnp.sum(inner.astype(f32), 0, keepdims=True)
            in_sum = block_sum if in_sum is None else in_sum + block_sum
        in_sum_ref[...] = in_sum
        part = dot_last(inner_ref[...], in_ref[0])

        @pl.when(tile == 0)
        def _():
            total_ref[...] = part + dot_last(logit_ref[...], router_ref[...])

        @pl.when(tile > 0)
        def _():
            total_ref[...] += part

    @pl.when((phase == 1) & (tile == tiles - 1))
    def _():
        back_ref[...] = total_ref[...].astype(bf16)


def expert_chunk(here, rows_in, cots, weights, router, experts):
    rows, width = rows_in.shape
    weight_in, bias_in, weight_out, bias_out = weights
    hidden = weight_in.shape[2]
    depth = 512
    tiles = hidden // depth

    def first_phase(p, f, _):
        return (0, jnp.where(p == 0, f, tiles - 1))

    def second_phase(p, f, _):
        return (0, jnp.where(p == 0, 0, f))

    every = whole((rows, width))

    def shape(columns):
        return jax.ShapeDtypeStruct((rows, columns), bf16)

    return pl.pallas_call(
        functools.partial(expert_kernel, experts, tiles),
        grid_spec=pltpu.PrefetchScalarGridSpec(
            num_scalar_prefetch=1,
            grid=(2, tiles),
            in_specs=[
                every,
                every,
                pl.BlockSpec((1, width, depth), lambda p, f, _: (0, 0, f)),
                pl.BlockSpec((1, depth), lambda p, f, _: (0, f)),
                pl.BlockSpec((1, depth, width), lambda p, f, _: (0, f, 0)),
                whole((1, width)),
                whole(router.shape),
            ],
            out_specs=[
                every,
                every,
                pl.BlockSpec((rows, depth), first_phase),
                pl.BlockSpec((rows, depth), second_phase),
                every,
                whole((rows, LANES)),
                pl.BlockSpec((1, depth), second_phase),
                whole((1, width)),
            ],
            scratch_shapes=[
                pltpu.VMEM((tiles, rows, depth), f32),
                pltpu.VMEM((rows, width), f32),
            ],
        ),
        out_shape=[
            shape(width),
            shape(width),
            shape(hidden),
            shape(hidden),
            shape(width),
            shape(LANES),
            jax.ShapeDtypeStruct((1, hidden), f32),
            jax.ShapeDtypeStruct((1, width), f32),
        ],
        compiler_params=params(2),
        cost_estimate=cost(),
        name="expert_chunk",
    )(here, rows_in, cots, weight_in, bias_in, weight_out, bias_out, router)


def out_grad_kernel(parts, core_ref, *refs):
    hidden_refs, outer_refs = refs[:parts], refs[parts : 2 * parts]
    mine_ref, other_ref = refs[2 * parts : 2 * parts + 2]
    turned_refs = refs[2 * parts + 2 :]
    step = pl.program_id(0)

    @pl.when(step == 0)
    def _():
        for outer_ref, turned_ref in zip(outer_refs, turned_refs):
            turned_ref[...] = outer_ref[...].T

    total = sum(dot(turned[...], hidden[...]) for turned, hidden in zip(turned_refs, hidden_refs))
    block = total.astype(bf16).T

    @pl.when(step < pl.num_programs(0) // 2)
    def _():
        other_ref[...] = block

    @pl.when(step >= pl.num_programs(0) // 2)
    def _():
        mine_ref[...] = block


def out_grad(core, hiddens, outers):
    parts = len(hiddens)
    high, wide = hiddens[0].shape[1], outers[0].shape[1]
    tile = 512
    half = high // 2 // tile

    def place(i, core_ref):
        own = i >= half
        return (0, jnp.where(own, core_ref[0], 1 - core_ref[0]) * half + i - own * half)

    return pl.pallas_call(
        functools.partial(out_grad_kernel, parts),
        grid_spec=pltpu.PrefetchScalarGridSpec(
            num_scalar_prefetch=1,
            grid=(2 * half,),
            in_specs=[pl.BlockSpec((rows.shape[0], tile), place) for rows in hiddens]
            + [whole(rows.shape) for rows in outers],
            out_specs=[
                pl.BlockSpec((tile, wide), lambda i, _: (jnp.maximum(i - half, 0), 0)),
                pl.BlockSpec((tile, wide), lambda i, _: (jnp.minimum(i, half - 1), 0)),
            ],
            scratch_shapes=[pltpu.VMEM((wide, rows.shape[0]), bf16) for rows in outers],
        ),
        out_shape=[jax.ShapeDtypeStruct((high // 2, wide), bf16)] * 2,
        compiler_params=params(1),
        cost_estimate=cost(),
        name="out_grad",
    )(core, *hiddens, *outers)


def in_grad_kernel(parts, core_ref, *refs):
    arrived_refs, inner_refs, logit_refs = (refs[i * parts : (i + 1) * parts] for i in range(3))
    mine_ref, other_ref, router_ref = refs[3 * parts : 3 * parts + 3]
    turned_refs = refs[3 * parts + 3 :]
    half = mine_ref.shape[0]

    @pl.when(pl.program_id(0) == 0)
    def _():
        for arrived_ref, turned_ref in zip(arrived_refs, turned_refs):
            turned = arrived_ref[...].T
            turned_ref[0] = turned[:half]
            turned_ref[1] = turned[half:]
        for h in range(2):
            router_ref[h * half : (h + 1) * half, :] = sum(
                dot(turned[h], logit[...]) for turned, logit in zip(turned_refs, logit_refs)
            )

    core = core_ref[0]
    mine_ref[...] = sum(
        dot(turned[core], inner[...]) for turned, inner in zip(turned_refs, inner_refs)
    ).astype(bf16)
    other_ref[...] = sum(
        dot(turned[1 - core], inner[...]) for turned, inner in zip(turned_refs, inner_refs)
    ).astype(bf16)


def in_grad(core, arrived, inners, logits):
    parts = len(inners)
    high, wide = arrived[0].shape[1], inners[0].shape[1]
    tile = 512
    spec = pl.BlockSpec((high // 2, tile), lambda i, _: (0, i))
    return pl.pallas_call(
        functools.partial(in_grad_kernel, parts),
        grid_spec=pltpu.PrefetchScalarGridSpec(
            num_scalar_prefetch=1,
            grid=(wide // tile,),
            in_specs=[whole(rows.shape) for rows in arrived]
            + [pl.BlockSpec((rows.shape[0], tile), lambda i, _: (0, i)) for rows in inners]
            + [whole(rows.shape) for rows in logits],
            out_specs=[spec, spec, whole((high, LANES))],
            scratch_shapes=[pltpu.VMEM((2, high // 2, rows.shape[0]), bf16) for rows in arrived],
        ),
        out_shape=[jax.ShapeDtypeStruct((high // 2, wide), bf16)] * 2
        + [jax.ShapeDtypeStruct((high, LANES), f32)],
        compiler_params=params(1),
        cost_estimate=cost(),
        name="in_grad",
    )(core, *arrived, *inners, *logits)


def widen_kernel(core_ref, mine_ref, theirs_ref, *refs):
    out_ref = refs[-1]
    own = pl.program_id(0) == core_ref[0]

    @pl.when(own)
    def _():
        out_ref[...] = mine_ref[...].astype(f32)

    @pl.when(jnp.logical_not(own))
    def _():
        out_ref[...] = theirs_ref[...].astype(f32)


def widen(core, mine, theirs, column=0, columns=1, kept=()):
    high, wide = mine.shape
    tile = high // 4

    def block(is_mine):
        def index(h, i, core_ref):
            used = (h == core_ref[0]) == is_mine
            return (jnp.where(used, i, 0), 0)

        return pl.BlockSpec((tile, wide), index)

    return pl.pallas_call(
        widen_kernel,
        grid_spec=pltpu.PrefetchScalarGridSpec(
            num_scalar_prefetch=1,
            grid=(2, 4),
            in_specs=[block(True), block(False)]
            + [pl.BlockSpec(memory_space=pl.ANY)] * len(kept),
            out_specs=pl.BlockSpec((tile, wide), lambda h, i, _: (h * 4 + i, column)),
        ),
        out_shape=jax.ShapeDtypeStruct((2 * high, columns * wide), f32),
        input_output_aliases={3: 0} if kept else {},
        compiler_params=params(2),
        cost_estimate=cost(),
        name="widen",
    )(core, mine, theirs, *kept)


def collect(slots, rows):
    slot = lax.broadcasted_iota(jnp.int32, (1, rows.shape[0]), 1)
    hot = (slots[:, 0:1] == slot) | (slots[:, 1:2] == slot)
    return dot(jnp.where(hot, 1.0, 0.0).astype(bf16), rows)


def collect_parts(slots, part_refs):
    return sum(
        collect(slots[:, 2 * part : 2 * part + 2], part_ref[...])
        for part, part_ref in enumerate(part_refs)
    )


def output_kernel(slot_ref, mid_ref, *refs):
    refs[-1][0] = (mid_ref[0] + collect_parts(slot_ref[0].T, refs[:-1])).astype(bf16)


def combine_output(image_slots, middle, returned):
    images, rows, width = middle.shape
    spec = pl.BlockSpec((1, rows, width), lambda i: (i, 0, 0))
    return pl.pallas_call(
        output_kernel,
        grid=(images,),
        in_specs=[pl.BlockSpec((1, *image_slots.shape[1:]), lambda i: (i, 0, 0)), spec]
        + [whole(part.shape) for part in returned],
        out_specs=spec,
        out_shape=jax.ShapeDtypeStruct((images, rows, width), bf16),
        compiler_params=params(1),
        cost_estimate=cost(),
        name="combine_output",
    )(image_slots, middle, *returned)


def backward_kernel(seq_len, width, experts, parts, core_ref, *refs):
    slot_ref, x_ref, cot_ref, mid_ref, qkv_ref, w_ref, vec_ref = refs[:7]
    h1_ref, o_ref, router_ref = refs[7:10]
    part_refs = refs[10 : 10 + parts]
    grad_ref, mine_ref, other_ref, dqkv_ref, sums_ref, total_ref = refs[10 + parts :]
    vec = vec_ref[...]

    def row(index):
        return vec[index : index + 1]

    h2_grad = collect_parts(slot_ref[0].T, part_refs)
    scaled, inverse = normalize(mid_ref[0])
    norm_grad, gain_two_grad, shift_two_grad = norm_back(h2_grad, scaled, inverse, row(GAIN_TWO))
    mid_grad = cot_ref[0].astype(f32) + norm_grad
    branch = mid_grad.astype(bf16)
    out_shift_grad = jnp.sum(branch.astype(f32), 0, keepdims=True)
    o_grad = dot_last(branch, w_ref[:, 3 * width : 4 * width]).astype(bf16)

    rows = branch.shape[0]
    lane = lax.broadcasted_iota(jnp.int32, (1, LANES), 1)
    key_there = lax.broadcasted_iota(jnp.int32, (rows, 1), 0) < seq_len
    factor = HEAD_DIM ** (-0.5)
    for pair in range(width // LANES):
        at = pair * LANES
        queries = qkv_ref[0, :, at : at + LANES] * jnp.asarray(factor, bf16)
        keys = qkv_ref[0, :, width + at : width + at + LANES]
        values = qkv_ref[0, :, 2 * width + at : 2 * width + at + LANES]
        grads = o_grad[:, at : at + LANES]
        query_grad = key_grad = value_grad = None
        for half in range(LANES // HEAD_DIM):
            mine = (lane // HEAD_DIM) == half

            def only(slab):
                return jnp.where(mine, slab, jnp.zeros_like(slab))

            own_queries, own_keys, own_grads = only(queries), only(keys), only(grads)
            scores = dot_last(own_keys, queries)
            scores = jnp.where(key_there, scores, -1e30)
            powers = jnp.exp(scores - jnp.max(scores, 0, keepdims=True))
            probs = powers * (1.0 / jnp.sum(powers, 0, keepdims=True))
            prob_grad = dot_last(values, own_grads)
            spread = jnp.sum(probs * prob_grad, 0, keepdims=True)
            score_grad = (probs * (prob_grad - spread)).astype(bf16)
            value_part = dot(probs.astype(bf16), own_grads)
            key_part = dot(score_grad, own_queries)
            query_part = dot_first(score_grad, own_keys)
            if half == 0:
                query_grad, key_grad, value_grad = query_part, key_part, value_part
            else:
                query_grad += query_part
                key_grad += key_part
                value_grad += value_part
        dqkv_ref[:, at : at + LANES] = (query_grad * factor).astype(bf16)
        dqkv_ref[:, width + at : width + at + LANES] = key_grad.astype(bf16)
        dqkv_ref[:, 2 * width + at : 2 * width + at + LANES] = value_grad.astype(bf16)

    h1_grad = dot_last(dqkv_ref[...], w_ref[:, : 3 * width])
    query_sum = jnp.sum(dqkv_ref[:, :width].astype(f32), 0, keepdims=True)
    value_sum = jnp.sum(dqkv_ref[:, 2 * width :].astype(f32), 0, keepdims=True)
    scaled, inverse = normalize(x_ref[0].astype(f32))
    norm_grad, gain_one_grad, shift_one_grad = norm_back(h1_grad, scaled, inverse, row(GAIN_ONE))
    grad_ref[0] = (mid_grad + norm_grad).astype(bf16)
    sums = [
        gain_one_grad,
        shift_one_grad,
        query_sum,
        value_sum,
        out_shift_grad,
        gain_two_grad,
        shift_two_grad,
        jnp.zeros((sums_ref.shape[0] - VECTORS, width), f32),
    ]
    sums = jnp.concatenate(sums, 0)

    image = pl.program_id(0)
    qkv_part = dot_first(h1_ref[0], dqkv_ref[...])
    out_part = dot_first(o_ref[0], branch)

    @pl.when(image == 0)
    def _():
        sums_ref[...] = sums
        total_ref[:, : 3 * width] = qkv_part
        total_ref[:, 3 * width : 4 * width] = out_part

    @pl.when(image > 0)
    def _():
        sums_ref[...] += sums
        total_ref[:, : 3 * width] += qkv_part
        total_ref[:, 3 * width : 4 * width] += out_part

    @pl.when(image == pl.num_programs(0) - 1)
    def _():
        small = total_ref.shape[1] - 4 * width
        column = lax.broadcasted_iota(jnp.int32, (8, small), 1)
        pick = jnp.where(column == experts + lax.broadcasted_iota(jnp.int32, (8, small), 0), 1.0, 0.0)
        total_ref[:, 4 * width :] = dot_first(sums_ref[...].astype(bf16), pick.astype(bf16))
        own = lax.broadcasted_iota(jnp.int32, (1, LANES), 1) < experts
        total_ref[:, 4 * width : 4 * width + LANES] += jnp.where(own, router_ref[...], 0.0)
        half = total_ref.shape[1] // 2

        @pl.when(core_ref[0] == 0)
        def _():
            mine_ref[...] = total_ref[:, :half].astype(bf16)
            other_ref[...] = total_ref[:, half:].astype(bf16)

        @pl.when(core_ref[0] != 0)
        def _():
            other_ref[...] = total_ref[:, :half].astype(bf16)
            mine_ref[...] = total_ref[:, half:].astype(bf16)


def attention_backward(
    core, image_slots, x, cot, middle, qkv, packed, vec, h1, attended, router_grad, back, experts, seq_len
):
    images, rows, width = x.shape
    columns = 4 * width + round_up(experts + VECTORS, 2 * LANES)

    def spec(columns):
        return pl.BlockSpec((1, rows, columns), lambda i: (i, 0, 0))

    half = jax.ShapeDtypeStruct((width, columns // 2), bf16)
    return pl.pallas_call(
        functools.partial(backward_kernel, seq_len, width, experts, len(back)),
        grid=(images,),
        in_specs=[
            scalar_spec(),
            pl.BlockSpec((1, *image_slots.shape[1:]), lambda i: (i, 0, 0)),
            spec(width),
            spec(width),
            spec(width),
            spec(3 * width),
            whole(packed.shape),
            whole(vec.shape),
            spec(width),
            spec(width),
            whole(router_grad.shape),
        ]
        + [whole(part.shape) for part in back],
        out_specs=[spec(width), whole(half.shape), whole(half.shape)],
        out_shape=[jax.ShapeDtypeStruct(x.shape, bf16), half, half],
        scratch_shapes=[
            pltpu.VMEM((rows, 3 * width), bf16),
            pltpu.VMEM((8, width), f32),
            pltpu.VMEM((width, columns), f32),
        ],
        compiler_params=params(1),
        cost_estimate=cost(),
        name="attention_backward",
    )(core, image_slots, x, cot, middle, qkv, packed, vec, h1, attended, router_grad, *back)


def swap(value, axis, distance):
    count = lax.axis_size(axis)
    return lax.ppermute(value, axis, [(i, i ^ distance) for i in range(count)])


def exchange(rows):
    experts = lax.axis_size("shard")
    blocks = rows.reshape(experts, rows.shape[0] // experts, rows.shape[1])
    moved = lax.all_to_all(blocks, "shard", split_axis=0, concat_axis=0, tiled=True)
    return moved.reshape(rows.shape)


def add(left, right):
    return (left.astype(f32) + right.astype(f32)).astype(bf16)


def halves(value, core, axis):
    half = value.shape[axis] // 2
    mine = lax.dynamic_slice_in_dim(value, core * half, half, axis)
    other = lax.dynamic_slice_in_dim(value, (1 - core) * half, half, axis)
    return mine, other


def join(mine, theirs, core, axis):
    first = jnp.where(core == 0, mine, theirs)
    second = jnp.where(core == 0, theirs, mine)
    return jnp.concatenate([first, second], axis)


def over_chips(value, step=2):
    while step < lax.axis_size("replica"):
        value = add(value, swap(value, "replica", step))
        step *= 2
    return value


def tie(*values):
    return lax.optimization_barrier(values)


def per_device(
    images,
    routes,
    cotangent,
    ln1_gain,
    ln1_bias,
    qkv_weight,
    q_bias,
    v_bias,
    out_weight,
    out_bias,
    ln2_gain,
    ln2_bias,
    router_weight,
    expert_in,
    expert_in_bias,
    expert_out,
    expert_out_bias,
):
    experts = lax.axis_size("shard")
    here = lax.axis_index("shard").reshape(1).astype(jnp.int32)
    core = lax.axis_index("replica") % 2
    images_here, seq_len, width = images.shape
    tokens_here = images_here * seq_len
    capacity = 14 * tokens_here // (5 * experts)
    first_part = round_up(-(-capacity // 2), 16)
    parts = [(0, first_part), (first_part, round_up(capacity - first_part, 8))]
    rows = round_up(seq_len, 16)
    tokens = images_here * rows

    columns = [ln1_gain, ln1_bias, q_bias, v_bias, out_bias, ln2_gain, ln2_bias]
    small = jnp.concatenate([router_weight, jnp.stack(columns, 1)], 1)
    small_width = round_up(small.shape[1], LANES)
    small = jnp.pad(small, ((0, 0), (0, small_width - small.shape[1])))
    shard = jnp.concatenate([qkv_weight, out_weight, small], 1)
    mine, _ = halves(shard, core, 0)
    mine = lax.all_gather(mine, "shard", axis=0, tiled=False)

    pad_rows = ((0, 0), (0, rows - seq_len), (0, 0))
    route_rows = jnp.pad(routes, pad_rows, constant_values=-1).reshape(tokens, 2).T
    expert_ids = jnp.arange(experts, dtype=jnp.int32)[:, None]
    named = (route_rows[0:1] == expert_ids) | (route_rows[1:2] == expert_ids)
    token = jnp.arange(tokens, dtype=jnp.int32)
    earlier = (token[:, None] < token[None, :]).astype(bf16)
    ranking = dot(named.astype(bf16), earlier).astype(jnp.int32)
    ranks = [
        jnp.sum(jnp.where(route_rows[j][None] == expert_ids, ranking, 0), 0) for j in range(2)
    ]
    there = route_rows[0] >= 0
    part_slots = [
        jnp.where(
            there & (ranks[j] >= first) & (ranks[j] < first + size),
            route_rows[j] * size + ranks[j] - first,
            -1,
        )
        for first, size in parts
        for j in range(2)
    ]
    part_rows = [jnp.stack(part_slots[2 * i : 2 * i + 2], 0) for i in range(len(parts))]
    image_slots = part_slots + part_slots[:1] * (8 - len(part_slots))
    image_slots = jnp.stack(image_slots, 0).reshape(8, images_here, rows).swapaxes(0, 1)

    def place(values):
        return [
            dispatch(part_rows[i], values, experts * size, 4) for i, (_, size) in enumerate(parts)
        ]

    x = jnp.pad(images, pad_rows)
    cot = jnp.pad(cotangent, pad_rows)
    cot_sent = place(cot.reshape(tokens, width))
    cot_there = [exchange(cot_sent[0])]
    mine, cot_there[0], cot_sent[1], x, cot, image_slots = tie(
        mine, cot_there[0], cot_sent[1], x, cot, image_slots
    )
    cot_there.append(exchange(cot_sent[1]))
    packed = join(mine, swap(mine, "replica", 1), core, 1).reshape(width, shard.shape[1])
    small_full = packed[:, 4 * width :]
    lane = jnp.arange(small_width, dtype=jnp.int32)[None, :]
    router = jnp.where(lane < experts, small_full, jnp.zeros_like(small_full))[:, :LANES]
    pick = (lane == experts + jnp.arange(8, dtype=jnp.int32)[:, None]).astype(bf16)
    vec = dot_last(pick, small_full)

    h1, qkv, attended, middle, h2 = attention_forward(x, packed, vec, seq_len)
    sent = place(h2.reshape(tokens, width))
    sent[0], cot_there[1] = tie(sent[0], cot_there[1])
    arrived = [exchange(sent[0])]
    sent[1], arrived[0] = tie(sent[1], arrived[0])
    arrived.append(exchange(sent[1]))

    weights = (expert_in, expert_in_bias, expert_out, expert_out_bias)
    first = expert_chunk(here, arrived[0], cot_there[0], weights, router, experts)
    back_first, arrived[1] = tie(first[0], arrived[1])
    back = [exchange(back_first)]
    second = expert_chunk(here, arrived[1], cot_there[1], weights, router, experts)
    back_second, back[0], *second = tie(second[0], back[0], *second[1:])
    back.append(exchange(back_second))
    gated, hiddens, inners, outers, logits, in_sums, out_sums = zip(first[1:], second)

    core_here = core.reshape(1).astype(jnp.int32)
    out_mine, out_other = out_grad(core_here, hiddens, outers)
    in_mine, in_other, router_grad = in_grad(core_here, arrived, inners, logits)
    back[1], out_mine, out_other, in_mine, in_other = tie(
        back[1], out_mine, out_other, in_mine, in_other
    )
    out_mine = add(out_mine, swap(out_other, "replica", 1))
    in_mine = add(in_mine, swap(in_other, "replica", 1))
    biases = jnp.concatenate([sum(in_sums)[0], sum(out_sums)[0]]).reshape(-1, width).astype(bf16)
    biases = over_chips(add(biases, swap(biases, "replica", 1)))
    out_theirs = swap(out_mine, "replica", 2)

    first_gated, back[1] = tie(gated[0], back[1])
    returned = [exchange(first_gated)]
    input_grad, mine, other = attention_backward(
        core_here,
        image_slots,
        x,
        cot,
        middle,
        qkv,
        packed,
        vec,
        h1,
        attended,
        router_grad,
        back,
        experts,
        seq_len,
    )
    mine, other, returned[0], out_theirs = tie(mine, other, returned[0], out_theirs)
    second_gated, returned[0] = tie(gated[1], returned[0])
    returned.append(exchange(second_gated))
    mine = add(mine, swap(other, "replica", 1)).reshape(experts, width // experts, -1)
    chip = lax.axis_index("replica") // 2 % 2
    mine, other = halves(mine, chip, 1)
    mine = add(mine, swap(other, "replica", 2))
    out_mine = over_chips(add(out_mine, out_theirs), 4)
    in_mine, mine = tie(in_mine, mine)
    half_wide = in_mine.shape[1] // 2
    in_first = over_chips(in_mine[:, :half_wide])
    in_second, in_first = tie(in_mine[:, half_wide:], in_first)
    in_second = over_chips(in_second)
    mine, returned[1] = tie(mine, returned[1])
    pieces = lax.all_to_all(mine, "shard", split_axis=0, concat_axis=0, tiled=True)
    output = combine_output(image_slots, middle, returned)
    expert_out_grad = widen(core_here, out_mine, swap(out_mine, "replica", 1))[None]
    in_wide = widen(core_here, in_first, swap(in_first, "replica", 1), 0, 2)
    pieces, output, expert_out_grad, in_wide = tie(pieces, output, expert_out_grad, in_wide)
    mine = jnp.sum(pieces.astype(f32), 0).astype(bf16)
    mine = over_chips(mine, 4)
    mine = join(mine, swap(mine, "replica", 2), chip, 0)
    summed = join(mine, swap(mine, "replica", 1), core, 1).astype(f32)

    in_theirs = swap(in_second, "replica", 1)
    expert_in_grad = widen(core_here, in_second, in_theirs, 1, 2, (in_wide,))[None]
    biases = biases.astype(f32).reshape(1, -1)
    hidden_width = expert_in_bias.shape[1]
    small_sum = summed[:, 4 * width :]
    vector_sums = small_sum[:, experts : experts + VECTORS].T
    return (
        output[:, :seq_len],
        input_grad[:, :seq_len],
        vector_sums[GAIN_ONE],
        vector_sums[SHIFT_ONE],
        summed[:, : 3 * width],
        vector_sums[QUERY_BIAS],
        vector_sums[VALUE_BIAS],
        summed[:, 3 * width : 4 * width],
        vector_sums[OUT_SHIFT],
        vector_sums[GAIN_TWO],
        vector_sums[SHIFT_TWO],
        small_sum[:, :experts],
        expert_in_grad,
        biases[:, :hidden_width],
        expert_out_grad,
        biases[:, hidden_width:],
    )


def solution(mesh):
    return jax.shard_map(
        per_device,
        mesh=mesh,
        in_specs=(
            P(("replica", "shard"), None, None),
            P(("replica", "shard"), None, None),
            P(("replica", "shard"), None, None),
            P("shard"),
            P("shard"),
            P("shard", None),
            P("shard"),
            P("shard"),
            P("shard", None),
            P("shard"),
            P("shard"),
            P("shard"),
            P("shard", None),
            P("shard", None, None),
            P("shard", None),
            P("shard", None, None),
            P("shard", None),
        ),
        out_specs=(
            P(("replica", "shard"), None, None),
            P(("replica", "shard"), None, None),
            P("shard"),
            P("shard"),
            P("shard", None),
            P("shard"),
            P("shard"),
            P("shard", None),
            P("shard"),
            P("shard"),
            P("shard"),
            P("shard", None),
            P("shard", None, None),
            P("shard", None),
            P("shard", None, None),
            P("shard", None),
        ),
        check_vma=False,
    )
```
